512 devices in a mesh: tm: 16 (over z), sta: 32 (over y, x, core).
Axes of the slice: x: 4, y: 4, z: 16, core: 2. Of those that a mesh axis runs over, the one named last changes fastest.
Arguments:
- ray_basis: bfloat16 [16, 32768, 256], P('tm', 'sta'), may hold values from -0.06629126 to 0.06629126
- delays: bfloat16 [16, 32768], P('tm', 'sta'), may hold values from -24 to 24
- ray_station: int32 [16, 32768], P('tm', 'sta'), may hold values from 0 to 511, as said below
- ray_count: int32 [16, 32], P('tm', 'sta'), may hold values from 128 to 1024, as said below
- station_var: float32 [512], P('sta'), may hold values from 0.25 to 4
- decay_factor: float32 [16, 256], P('tm'), may hold values from 0.02 to 0.995, as said below
- mode_variance: float32 [256], replicated, may hold values from 0.3 to 3
- prior_mean: float32 [256], replicated, may hold values from -6 to 6
Outputs:
- smoothed: float32 [16, 256], P('tm')
The draws below stay inside these ranges and needn't reach their ends.
Inputs may be any that keep to these rules, and one draw needn't show every extreme that they name: `ray_station`: each ray's station is one of the 16 stations of the station shard that holds the ray. `ray_count`: each entry is a multiple of 128; the live slots of a shard come first; some shard is full in every draw. `decay_factor`: each entry lies strictly between 0 and 1.
All inputs are finite; a program needn't handle non-finite values.
Results may differ from the reference program's by a relative error of at most 0.005.
Values sent between devices are 32-bit elements; how exact they have to be, the bound alone decides.
No kernel may reach another device: no remote copies, remote signals or barrier semaphores. Data moves between devices by JAX's collectives and lax.ppermute only.
A program may use at most 64 MiB of HBM per device.

```python
import math
import jax
import jax.numpy as jnp
from jax import lax

STATE = 256
RAY_DEV = 1024
STA_DEV = 16
TOTAL_EPOCHS = 16
RAYS = 32768
STATIONS = 512
STA_SHARDS = 32


def draw_ray_basis(key, part):
    first_key = jax.random.fold_in(jax.random.fold_in(key, 11), 0)
    base = jnp.clip(jax.random.normal(first_key, (TOTAL_EPOCHS, RAYS, STATE), jnp.float32), -6.0, 6.0)
    mixed = base + 0.7 * jnp.roll(base, 1, axis=2) + 0.5 * jnp.roll(base, 7, axis=2)
    return (mixed * (0.45 / math.sqrt(RAYS))).astype(jnp.bfloat16)


def draw_ray_station(key, part):
    local_station = jax.random.randint(jax.random.fold_in(key, 23), (TOTAL_EPOCHS, RAYS), 0, STA_DEV, dtype=jnp.int32)
    shard_index = jnp.arange(RAYS, dtype=jnp.int32) // RAY_DEV
    return shard_index[None, :] * STA_DEV + local_station


def draw_ray_count(key, part):
    divided_keys = jax.random.split(jax.random.fold_in(key, 37), 3)
    blocks = jax.random.randint(divided_keys[0], (TOTAL_EPOCHS, STA_SHARDS), 1, RAY_DEV // 128 + 1, dtype=jnp.int32)
    full_row = jax.random.randint(divided_keys[1], (), 0, TOTAL_EPOCHS, dtype=jnp.int32)
    full_column = jax.random.randint(divided_keys[2], (), 0, STA_SHARDS, dtype=jnp.int32)
    counts = blocks * 128
    return counts.at[full_row, full_column].set(RAY_DEV)


def draw_decay_factor(key, part):
    divided_keys = jax.random.split(jax.random.fold_in(key, 51), 4)
    lowest = math.log(1.0 / (4 * TOTAL_EPOCHS))
    highest = math.log(2.0)
    base_rate = jnp.exp(jax.random.uniform(divided_keys[0], (1, STATE), jnp.float32, lowest, highest))
    factor = jnp.exp(jax.random.uniform(divided_keys[1], (TOTAL_EPOCHS, STATE), jnp.float32, -0.35, 0.35))
    damped_value = jnp.exp(-base_rate * factor)
    outburst_rows = jax.random.randint(divided_keys[2], (3,), 1, TOTAL_EPOCHS, dtype=jnp.int32)
    epoch_position_index = jnp.arange(TOTAL_EPOCHS, dtype=jnp.int32)
    outburst_flag = jnp.any(epoch_position_index[:, None] == outburst_rows[None, :], axis=1)
    outburst_magnitude = jax.random.uniform(divided_keys[3], (TOTAL_EPOCHS, STATE), jnp.float32, 0.5, 0.8)
    return jnp.where(outburst_flag[:, None], damped_value * outburst_magnitude, damped_value)


def level_of(key, extent, pieces, low, largest):
    factor_of = 1.0
    for dim, shards_of in pieces:
        heights = jax.random.uniform(jax.random.fold_in(jax.random.fold_in(key, 6), dim), (shards_of,), jnp.float32, low / len(pieces), largest / len(pieces))
        factor_of = factor_of * jnp.repeat(jnp.exp(heights), extent[dim] // shards_of).reshape((-1,) + (1,) * (len(extent) - 1 - dim))
    return factor_of


def bell_draw(own_key, dims, deviation, most, pieces=(), held_as=jnp.bfloat16):
    drawn = deviation * jax.random.normal(own_key, dims, jnp.float32)
    if pieces:
        drawn = drawn * level_of(own_key, dims, pieces, -0.22, 0.18)
    return jnp.clip(drawn, -most, most).astype(held_as)


def setup_inputs(seed: int = 0) -> dict:
    seeds = jax.random.split(jax.random.key(seed), 9)
    return {
        "ray_basis": draw_ray_basis(jax.random.fold_in(seeds[8], 71), 0),
        "delays": bell_draw(seeds[1], (TOTAL_EPOCHS, RAYS), 4.0, 24.0, ((0, 16), (1, 32))),
        "ray_station": draw_ray_station(jax.random.fold_in(seeds[8], 71), 0),
        "ray_count": draw_ray_count(jax.random.fold_in(seeds[8], 71), 0),
        "station_var": jnp.clip(jnp.exp(math.log(4.0) - 2.7725887 * jax.random.uniform(seeds[4], (STATIONS,), jnp.float32) ** level_of(seeds[4], (STATIONS,), ((0, 32),), -0.2, 0.2)), 0.25, 4.0),
        "decay_factor": draw_decay_factor(jax.random.fold_in(seeds[8], 71), 0),
        "mode_variance": jnp.clip(jnp.exp(jax.random.uniform(seeds[6], (STATE,), jnp.float32, math.log(0.3), math.log(3.0))), 0.3, 3.0),
        "prior_mean": bell_draw(seeds[7], (STATE,), 1.0, 6.0, (), jnp.float32),
    }


PRECISE = lax.Precision.HIGHEST

def product(left, right):
    return jnp.dot(left, right, precision=PRECISE)

def spd_inverse(matrix):
    lower_factor = jnp.linalg.cholesky(matrix)
    identity = jnp.eye(matrix.shape[0], dtype=matrix.dtype)
    inverse = jax.scipy.linalg.cho_solve((lower_factor, True), identity)
    return 0.5 * (inverse + inverse.T)

def kalman_update(mean_prev, info_prev, decay_row, noise_row, information, drive_vector, is_first):
    inverse_noise = 1.0 / noise_row
    scaled = decay_row * inverse_noise
    identity = jnp.eye(noise_row.shape[0], dtype=jnp.float32)
    inner = jnp.where(is_first, identity, info_prev + jnp.diag(decay_row * scaled))
    kernel = spd_inverse(inner)
    pred_info = jnp.diag(inverse_noise) - jnp.where(is_first, 0.0, scaled[:, None] * kernel * scaled[None, :])
    info_new = pred_info + information
    info_new = 0.5 * (info_new + info_new.T)
    target = product(pred_info, decay_row * mean_prev) + drive_vector
    factor = jnp.linalg.cholesky(info_new)
    mean_new = jax.scipy.linalg.cho_solve((factor, True), target)
    return (mean_new, info_new)

def reference(ray_basis, delays, ray_station, ray_count, station_var, decay_factor, mode_variance, prior_mean):
    slot_index = jnp.arange(RAYS, dtype=jnp.int32)
    shard_index = slot_index // RAY_DEV
    within_shard = slot_index - shard_index * RAY_DEV
    process_noise = (1.0 - decay_factor * decay_factor) * mode_variance[None, :]

    def one_epoch(epoch_items):
        basis, delay_row, station_row, count_row = epoch_items
        live_slot = within_shard < count_row[shard_index]
        weight = jnp.where(live_slot, 1.0 / station_var[station_row], 0.0)
        weighted = (basis.astype(jnp.float32) * weight[:, None]).astype(jnp.bfloat16)
        information = jnp.dot(weighted.T.astype(jnp.float32), basis.astype(jnp.float32), preferred_element_type=jnp.float32)
        drive_vector = jnp.dot(delay_row.astype(jnp.float32), weighted.astype(jnp.float32), preferred_element_type=jnp.float32)
        return (information, drive_vector)
    informations, drives = lax.map(one_epoch, (ray_basis, delays, ray_station, ray_count))
    first_flags = jnp.arange(TOTAL_EPOCHS, dtype=jnp.int32) == 0

    def forward(carried, epoch_items):
        information, drive_vector, decay_row, noise_row, is_first = epoch_items
        mean_new, info_new = kalman_update(carried[0], carried[1], decay_row, noise_row, information, drive_vector, is_first)
        return ((mean_new, info_new), (mean_new, info_new))
    start = (prior_mean, jnp.eye(STATE, dtype=jnp.float32))
    _, (filtered, filter_infos) = lax.scan(forward, start, (informations, drives, decay_factor, process_noise, first_flags))
    covariances = lax.map(spd_inverse, filter_infos)

    def backward(adjoint, epoch_items):
        mean_f, cov_f, information, drive_vector, decay_row = epoch_items
        smooth = mean_f + product(cov_f, adjoint)
        adjoint_prev = decay_row * (adjoint + drive_vector - product(information, smooth))
        return (adjoint_prev, smooth)
    _, smoothed = lax.scan(backward, jnp.zeros((STATE,), jnp.float32), (filtered, covariances, informations, drives, decay_factor), reverse=True)
    return smoothed
```

```python
import functools
import jax
import jax.numpy as jnp
from jax import lax
from jax.experimental import pallas as pl
from jax.experimental.pallas import tpu as pltpu
from jax.sharding import PartitionSpec as P

HALF = 128
TILE = 8
TOLERANCE = 1e-5
MOST_STEPS = 4000


def ray_kernel(
    spot_ref, count_ref, var_ref, basis_ref, delay_ref, station_ref, decay_ref, out_ref, weighted
):
    rays = basis_ref.shape[1]
    stations = var_ref.shape[0]
    shard = spot_ref[0]
    local = station_ref[...] - shard * stations
    variance = jnp.ones(local.shape, jnp.float32)
    for k in range(stations):
        variance = jnp.where(local == k, var_ref[k], variance)
    slot = lax.broadcasted_iota(jnp.int32, local.shape, 1)
    weight = jnp.where(slot < count_ref[0, 0], 1.0 / variance, 0.0)
    for start in range(0, rays, HALF):
        rows = slice(start, start + HALF)
        column = jnp.broadcast_to(weight[:, rows], (HALF, HALF)).T
        for lane in (0, HALF):
            lanes = slice(lane, lane + HALF)
            block = basis_ref[0, rows, lanes].astype(jnp.float32)
            weighted[rows, lanes] = (block * column).astype(jnp.bfloat16)
    scaled = weighted[...]
    information = lax.dot_general(
        scaled, basis_ref[0], (((0,), (0,)), ((), ())), preferred_element_type=jnp.float32
    )
    drive = jnp.dot(delay_ref[...], scaled, preferred_element_type=jnp.float32)
    first = information[:HALF, :HALF]
    second = information[HALF:, HALF:]
    row = lax.broadcasted_iota(jnp.int32, (HALF, HALF), 0)
    col = lax.broadcasted_iota(jnp.int32, (HALF, HALF), 1)
    diagonal = jnp.sum(jnp.where(row == col, second, 0.0), axis=0, keepdims=True)
    triangles = jnp.where(col >= row, first, second)
    groups = HALF // TILE
    shape = (groups, TILE, HALF)
    out_ref[:groups, :TILE, :] = triangles.reshape(shape)
    out_ref[groups:, :TILE, :] = information[:HALF, HALF:].reshape(shape)
    out_ref[:, TILE:, :] = jnp.zeros((2 * groups, TILE, HALF), jnp.float32)
    own = jnp.where(shard == 0, decay_ref[...], 0.0)
    extras = (drive[:, :HALF], drive[:, HALF:], diagonal, own[:, :HALF], own[:, HALF:])
    for k, extra in enumerate(extras):
        out_ref[k, TILE : TILE + 1, :] = extra


def sum_kernel(parts_ref, out_ref):
    total = jnp.sum(parts_ref[...], axis=0)
    for k in range(out_ref.shape[0]):
        out_ref[k] = total


def solve_kernel(
    spot_ref,
    mine_ref,
    other_ref,
    spread_ref,
    prior_ref,
    out_ref,
    packed,
    high,
    low,
    response,
):
    epochs, _, width = response.shape
    chips = mine_ref.shape[0]
    core = spot_ref[0]
    epoch_here = spot_ref[1]
    row = lax.broadcasted_iota(jnp.int32, (HALF, HALF), 0)
    col = lax.broadcasted_iota(jnp.int32, (HALF, HALF), 1)

    def unpack(e, carry):
        place = pl.multiple_of(e * TILE, TILE)
        for j in range(chips):
            ours = pl.multiple_of(2 * j * TILE + core * TILE, TILE)
            theirs = pl.multiple_of(2 * j * TILE + (1 - core) * TILE, TILE)
            packed[pl.ds(ours, TILE), :] = mine_ref[j, pl.ds(place, TILE), :]
            packed[pl.ds(theirs, TILE), :] = other_ref[j, pl.ds(place, TILE), :]
        triangles = packed[:HALF, :]
        corner = packed[HALF:, :]
        turned = triangles.T
        on_diagonal = row == col
        own = jnp.sum(jnp.where(on_diagonal, triangles, 0.0), axis=0, keepdims=True)
        first = jnp.where(on_diagonal, 0.0, jnp.where(col > row, triangles, turned))
        second = jnp.where(on_diagonal, 0.0, jnp.where(col < row, triangles, turned))
        base = pl.multiple_of(e * width, width)
        for r, c, block in ((0, 0, first), (0, 1, corner), (1, 0, corner.T), (1, 1, second)):
            rows = pl.ds(base + r * HALF, HALF)
            lanes = slice(c * HALF, c * HALF + HALF)
            upper = block.astype(jnp.bfloat16)
            high[rows, lanes] = upper
            low[rows, lanes] = (block - upper.astype(jnp.float32)).astype(jnp.bfloat16)
        return jnp.where(epoch_rows == e, own, carry)

    epoch_rows = lax.broadcasted_iota(jnp.int32, (epochs, HALF), 0)
    corner_diagonal = lax.fori_loop(0, epochs, unpack, jnp.zeros((epochs, HALF), jnp.float32))

    def extra(k):
        rows = slice(epochs * TILE, epochs * TILE + epochs)
        return jnp.where(core == k % 2, mine_ref[k // 2, rows, :], other_ref[k // 2, rows, :])

    drive = jnp.concatenate([extra(0), extra(1)], axis=1)
    decay = jnp.concatenate([extra(3), extra(4)], axis=1)
    diagonal = jnp.concatenate([corner_diagonal, extra(2)], axis=1)
    inverse_noise = 1.0 / ((1.0 - decay * decay) * spread_ref[...])
    index = lax.broadcasted_iota(jnp.int32, (epochs, width), 0)
    pull = decay * inverse_noise
    link_back = jnp.where(index == 0, 0.0, pull)
    link = jnp.where(index == epochs - 1, 0.0, pltpu.roll(pull, epochs - 1, 0))
    carried = jnp.where(index == epochs - 1, 0.0, pltpu.roll(decay * pull, epochs - 1, 0))
    middle = inverse_noise + carried + diagonal
    right = drive + jnp.where(index == 0, pull * prior_ref[...], 0.0)

    at = lambda x, e: x[e : e + 1, :]
    ahead = [at(middle, 0)]
    up = []
    for e in range(epochs - 1):
        up.append(at(link, e) / ahead[e])
        ahead.append(at(middle, e + 1) - at(link, e) * up[e])
    behind = at(middle, epochs - 1)
    down = [None] * epochs
    centre = [None] * epochs
    centre[epochs - 1] = 1.0 / ahead[epochs - 1]
    for e in reversed(range(epochs - 1)):
        down[e] = at(link, e) / behind
        reduced = at(link, e) * down[e]
        behind = at(middle, e) - reduced
        centre[e] = 1.0 / (ahead[e] - reduced)
    below = jnp.zeros((epochs, width), jnp.float32)
    for e in range(epochs):
        if e:
            below = below * down[e - 1]
        below = jnp.where(index == e, centre[e], below)
        response[e] = below
    above = jnp.where(index == epochs - 1, centre[epochs - 1], 0.0)
    for e in reversed(range(epochs - 1)):
        above = above * up[e]
        response[e] = response[e] + above
        above = jnp.where(index == e, centre[e], above)

    def precondition(r):
        total = at(r, 0) * response[0]
        for e in range(1, epochs):
            total = total + at(r, e) * response[e]
        return total

    def apply(p):
        blocks = []
        for e in range(epochs):
            kept = jnp.where(index == e, p, 0.0)
            upper = kept.astype(jnp.bfloat16)
            rest = (kept - upper.astype(jnp.float32)).astype(jnp.bfloat16)
            blocks.append(jnp.concatenate([upper, rest], axis=0))
        left = jnp.concatenate(blocks, axis=1)
        by_high = jnp.dot(left, high[...], preferred_element_type=jnp.float32)
        by_low = jnp.dot(left[:epochs], low[...], preferred_element_type=jnp.float32)
        near = (
            middle * p
            - link * pltpu.roll(p, epochs - 1, 0)
            - link_back * pltpu.roll(p, 1, 0)
        )
        return near + (by_high[:epochs] + by_high[epochs:] + by_low)

    def inner(a, b):
        return jnp.sum(jnp.sum(a * b, axis=0, keepdims=True), axis=1, keepdims=True)

    start = precondition(right)
    size = inner(right, start)
    bound = size[0, 0] * (TOLERANCE * TOLERANCE)

    def unfinished(state):
        return jnp.logical_and(state[0] < MOST_STEPS, state[5][0, 0] > bound)

    def step(state):
        count, x, r, p, _, size = state
        image = apply(p)
        energy = inner(p, image)
        length = jnp.where(energy > 0.0, size / energy, 0.0)
        x = x + length * p
        r = r - length * image
        z = precondition(r)
        fresh = inner(r, z)
        ratio = jnp.where(size > 0.0, fresh / size, 0.0)
        p = z + ratio * p
        return (count + 1, x, r, p, z, fresh)

    zero = jnp.zeros((epochs, width), jnp.float32)
    state = lax.while_loop(unfinished, step, (0, zero, right, start, zero, size))
    solved = state[1]
    out_ref[...] = jnp.sum(jnp.where(index == epoch_here, solved, 0.0), axis=0, keepdims=True)


VMEM = pl.BlockSpec(memory_space=pltpu.VMEM)
SMEM = pl.BlockSpec(memory_space=pltpu.SMEM)


def solve(spot, mine, other, spread, prior, epochs, width):
    return pl.pallas_call(
        solve_kernel,
        out_shape=jax.ShapeDtypeStruct((1, width), jnp.float32),
        in_specs=[SMEM, VMEM, VMEM, VMEM, VMEM],
        out_specs=VMEM,
        scratch_shapes=[
            pltpu.VMEM((width, HALF), jnp.float32),
            pltpu.VMEM((epochs * width, width), jnp.bfloat16),
            pltpu.VMEM((epochs * width, width), jnp.bfloat16),
            pltpu.VMEM((epochs, epochs, width), jnp.float32),
        ],
        compiler_params=pltpu.CompilerParams(vmem_limit_bytes=48 * 2**20),
    )(spot, mine, other, spread, prior)


def shards(
    ray_basis, delays, ray_station, ray_count, station_var, decay_factor, mode_variance, prior_mean
):
    rays, width = ray_basis.shape[1:]
    epochs = lax.axis_size("tm")
    parts = lax.axis_size("sta")
    chips = parts // 2
    shard = lax.axis_index("sta")
    core = lax.rem(shard, 2)
    slab = 2 * TILE
    share = pl.pallas_call(
        ray_kernel,
        out_shape=jax.ShapeDtypeStruct((parts, slab, HALF), jnp.float32),
        in_specs=[SMEM, SMEM, SMEM, VMEM, VMEM, VMEM, VMEM],
        out_specs=VMEM,
        scratch_shapes=[pltpu.VMEM((rays, width), jnp.bfloat16)],
        compiler_params=pltpu.CompilerParams(vmem_limit_bytes=32 * 2**20),
    )(shard[None], ray_count, station_var, ray_basis, delays, ray_station, decay_factor)
    spread = lax.all_to_all(share, "sta", split_axis=0, concat_axis=0, tiled=True)
    copies = pl.pallas_call(
        sum_kernel,
        out_shape=jax.ShapeDtypeStruct((epochs, slab, HALF), jnp.float32),
        in_specs=[VMEM],
        out_specs=VMEM,
    )(spread)
    rows = lax.all_to_all(copies, "tm", split_axis=0, concat_axis=0, tiled=True)
    ours = jnp.concatenate([rows[:, :TILE].reshape(epochs * TILE, HALF), rows[:, TILE]], axis=0)
    same_core = [[2 * j + c for j in range(chips)] for c in range(2)]
    mine = lax.all_to_all(
        jnp.broadcast_to(ours[None], (chips,) + ours.shape),
        "sta",
        split_axis=0,
        concat_axis=0,
        tiled=True,
        axis_index_groups=same_core,
    )
    other = lax.ppermute(mine, "sta", [(i, i + 1 - 2 * (i % 2)) for i in range(parts)])
    spot = jnp.stack([core, lax.axis_index("tm")])
    return solve(spot, mine, other, mode_variance[None], prior_mean[None], epochs, width)


def solution(mesh):
    placed = (
        P("tm", "sta", None),
        P("tm", "sta"),
        P("tm", "sta"),
        P("tm", "sta"),
        P("sta"),
        P("tm", None),
        P(),
        P(),
    )
    return jax.shard_map(
        shards, mesh=mesh, in_specs=placed, out_specs=P("tm", None), check_vma=False
    )
```

```python
import jax
import jax.numpy as jnp
from jax import lax
from jax.experimental import pallas as pl
from jax.experimental.pallas import tpu as pltpu
from jax.sharding import PartitionSpec as P

HALF = 128
TILE = 8
SLAB = TILE + 1
TOLERANCE = 1e-5
MOST_STEPS = 4000


def ray_kernel(
    count_hbm,
    var_hbm,
    basis_hbm,
    delay_hbm,
    station_hbm,
    decay_hbm,
    out_ref,
    count_ref,
    var_ref,
    basis_ref,
    delay_ref,
    station_ref,
    decay_ref,
    weighted,
    arrived,
):
    rays = basis_ref.shape[0]
    stations = var_ref.shape[0]
    small = [
        pltpu.make_async_copy(source, target, arrived.at[k])
        for k, (source, target) in enumerate(
            (
                (station_hbm, station_ref),
                (var_hbm, var_ref),
                (count_hbm, count_ref),
                (delay_hbm, delay_ref),
                (decay_hbm, decay_ref),
            )
        )
    ]
    whole = pltpu.make_async_copy(basis_hbm.at[0], basis_ref, arrived.at[len(small)])
    for copy in small:
        copy.start()
    whole.start()
    shard = lax.axis_index("sta")
    for copy in small:
        copy.wait()
    local = station_ref[...] - shard * stations
    variance = jnp.ones(local.shape, jnp.float32)
    for k in range(stations):
        variance = jnp.where(local == k, var_ref[k], variance)
    slot = lax.broadcasted_iota(jnp.int32, local.shape, 1)
    weight = jnp.where(slot < count_ref[0, 0], 1.0 / variance, 0.0)
    whole.wait()
    for start in range(0, rays, HALF):
        rows = slice(start, start + HALF)
        column = jnp.broadcast_to(weight[:, rows], (HALF, HALF)).T
        for lane in (0, HALF):
            lanes = slice(lane, lane + HALF)
            block = basis_ref[rows, lanes].astype(jnp.float32)
            weighted[rows, lanes] = (block * column).astype(jnp.bfloat16)
    scaled = weighted[...]
    information = lax.dot_general(
        scaled, basis_ref[...], (((0,), (0,)), ((), ())), preferred_element_type=jnp.float32
    )
    drive = jnp.dot(delay_ref[...], scaled, preferred_element_type=jnp.float32)
    first = information[:HALF, :HALF]
    second = information[HALF:, HALF:]
    row = lax.broadcasted_iota(jnp.int32, (HALF, HALF), 0)
    col = lax.broadcasted_iota(jnp.int32, (HALF, HALF), 1)
    diagonal = jnp.sum(jnp.where(row == col, second, 0.0), axis=0, keepdims=True)
    triangles = jnp.where(col >= row, first, second)
    corner = information[:HALF, HALF:]
    own = jnp.where(shard == 0, decay_ref[...], 0.0)
    extras = [drive[:, :HALF], drive[:, HALF:], diagonal, own[:, :HALF], own[:, HALF:]]
    blank = jnp.zeros((1, HALF), jnp.float32)
    for j in range(HALF // TILE):
        extra = extras[j] if j < len(extras) else blank
        for c, block in ((0, triangles), (1, corner)):
            base = (2 * j + c) * SLAB
            out_ref[base : base + TILE, 0, :] = block[j * TILE : j * TILE + TILE, :]
            out_ref[base + TILE, :, :] = extra


def sum_kernel(parts_ref, out_ref):
    total = parts_ref[0:TILE, 0, :]
    extra = parts_ref[TILE, :, :]
    for k in range(1, parts_ref.shape[0] // SLAB):
        base = k * SLAB
        total = total + parts_ref[base : base + TILE, 0, :]
        extra = extra + parts_ref[base + TILE, :, :]
    for k in range(out_ref.shape[0] // SLAB):
        base = k * SLAB
        out_ref[base : base + TILE, 0, :] = total
        out_ref[base + TILE, :, :] = extra


def copy_kernel(rows_ref, out_ref):
    epochs = rows_ref.shape[0] // SLAB
    for k in range(epochs):
        tile = rows_ref[k * SLAB : k * SLAB + TILE, 0, :]
        extra = rows_ref[k * SLAB + TILE, :, :]
        for j in range(out_ref.shape[0]):
            out_ref[j, k * TILE : k * TILE + TILE, :] = tile
            out_ref[j, epochs * TILE + k : epochs * TILE + k + 1, :] = extra


def solve_kernel(
    mine_ref,
    other_ref,
    spread_ref,
    prior_ref,
    out_ref,
    packed,
    high,
    low,
    response,
):
    epochs, _, width = response.shape
    chips = mine_ref.shape[0]
    core = lax.rem(lax.axis_index("sta"), 2)
    epoch_here = lax.axis_index("tm")
    row = lax.broadcasted_iota(jnp.int32, (HALF, HALF), 0)
    col = lax.broadcasted_iota(jnp.int32, (HALF, HALF), 1)

    def unpack(e, carry):
        place = pl.multiple_of(e * TILE, TILE)
        for j in range(chips):
            ours = pl.multiple_of(core * HALF + j * TILE, TILE)
            theirs = pl.multiple_of((1 - core) * HALF + j * TILE, TILE)
            packed[pl.ds(ours, TILE), :] = mine_ref[j, pl.ds(place, TILE), :]
            packed[pl.ds(theirs, TILE), :] = other_ref[j, pl.ds(place, TILE), :]
        triangles = packed[:HALF, :]
        corner = packed[HALF:, :]
        turned = triangles.T
        on_diagonal = row == col
        own = jnp.sum(jnp.where(on_diagonal, triangles, 0.0), axis=0, keepdims=True)
        first = jnp.where(on_diagonal, 0.0, jnp.where(col > row, triangles, turned))
        second = jnp.where(on_diagonal, 0.0, jnp.where(col < row, triangles, turned))
        base = pl.multiple_of(e * width, width)
        for r, c, block in ((0, 0, first), (0, 1, corner), (1, 0, corner.T), (1, 1, second)):
            rows = pl.ds(base + r * HALF, HALF)
            lanes = slice(c * HALF, c * HALF + HALF)
            upper = block.astype(jnp.bfloat16)
            high[rows, lanes] = upper
            low[rows, lanes] = (block - upper.astype(jnp.float32)).astype(jnp.bfloat16)
        return jnp.where(epoch_rows == e, own, carry)

    epoch_rows = lax.broadcasted_iota(jnp.int32, (epochs, HALF), 0)
    corner_diagonal = lax.fori_loop(0, epochs, unpack, jnp.zeros((epochs, HALF), jnp.float32))

    def extra(k):
        return mine_ref[k, epochs * TILE : epochs * TILE + epochs, :]

    drive = jnp.concatenate([extra(0), extra(1)], axis=1)
    decay = jnp.concatenate([extra(3), extra(4)], axis=1)
    diagonal = jnp.concatenate([corner_diagonal, extra(2)], axis=1)
    inverse_noise = 1.0 / ((1.0 - decay * decay) * spread_ref[...])
    index = lax.broadcasted_iota(jnp.int32, (epochs, width), 0)
    pull = decay * inverse_noise
    link_back = jnp.where(index == 0, 0.0, pull)
    link = jnp.where(index == epochs - 1, 0.0, pltpu.roll(pull, epochs - 1, 0))
    carried = jnp.where(index == epochs - 1, 0.0, pltpu.roll(decay * pull, epochs - 1, 0))
    middle = inverse_noise + carried + diagonal
    right = drive + jnp.where(index == 0, pull * prior_ref[...], 0.0)

    at = lambda x, e: x[e : e + 1, :]
    ahead = [at(middle, 0)]
    up = []
    for e in range(epochs - 1):
        up.append(at(link, e) / ahead[e])
        ahead.append(at(middle, e + 1) - at(link, e) * up[e])
    behind = at(middle, epochs - 1)
    down = [None] * epochs
    centre = [None] * epochs
    centre[epochs - 1] = 1.0 / ahead[epochs - 1]
    for e in reversed(range(epochs - 1)):
        down[e] = at(link, e) / behind
        reduced = at(link, e) * down[e]
        behind = at(middle, e) - reduced
        centre[e] = 1.0 / (ahead[e] - reduced)
    below = jnp.zeros((epochs, width), jnp.float32)
    for e in range(epochs):
        if e:
            below = below * down[e - 1]
        below = jnp.where(index == e, centre[e], below)
        response[e] = below
    above = jnp.where(index == epochs - 1, centre[epochs - 1], 0.0)
    for e in reversed(range(epochs - 1)):
        above = above * up[e]
        response[e] = response[e] + above
        above = jnp.where(index == e, centre[e], above)

    def precondition(r):
        total = at(r, 0) * response[0]
        for e in range(1, epochs):
            total = total + at(r, e) * response[e]
        return total

    def apply(p):
        blocks = []
        for e in range(epochs):
            kept = jnp.where(index == e, p, 0.0)
            upper = kept.astype(jnp.bfloat16)
            rest = (kept - upper.astype(jnp.float32)).astype(jnp.bfloat16)
            blocks.append(jnp.concatenate([upper, rest], axis=0))
        left = jnp.concatenate(blocks, axis=1)
        by_high = jnp.dot(left, high[...], preferred_element_type=jnp.float32)
        by_low = jnp.dot(left[:epochs], low[...], preferred_element_type=jnp.float32)
        near = (
            middle * p
            - link * pltpu.roll(p, epochs - 1, 0)
            - link_back * pltpu.roll(p, 1, 0)
        )
        return near + (by_high[:epochs] + by_high[epochs:] + by_low)

    def inner(a, b):
        return jnp.sum(jnp.sum(a * b, axis=0, keepdims=True), axis=1, keepdims=True)

    start = precondition(right)
    size = inner(right, start)
    bound = size[0, 0] * (TOLERANCE * TOLERANCE)

    def unfinished(state):
        return jnp.logical_and(state[0] < MOST_STEPS, state[6][0, 0] > bound)

    def step(state):
        count, x, r, z, p, path, size, before, length = state
        image = apply(z)
        energy = inner(z, image)
        ratio = jnp.where(before > 0.0, size / before, 0.0)
        past = jnp.where(length > 0.0, ratio * size / length, 0.0)
        energy = energy - past
        length = jnp.where(energy > 0.0, size / energy, 0.0)
        p = z + ratio * p
        path = image + ratio * path
        x = x + length * p
        r = r - length * path
        z = precondition(r)
        return (count + 1, x, r, z, p, path, inner(r, z), size, length)

    zero = jnp.zeros((epochs, width), jnp.float32)
    none = jnp.zeros((1, 1), jnp.float32)
    state = (0, zero, right, start, zero, zero, size, none, none)
    solved = lax.while_loop(unfinished, step, state)[1]
    out_ref[...] = jnp.sum(jnp.where(index == epoch_here, solved, 0.0), axis=0, keepdims=True)


VMEM = pl.BlockSpec(memory_space=pltpu.VMEM)
HBM = pl.BlockSpec(memory_space=pltpu.HBM)
MIB = 2**20


def call(kernel, shape, specs, scratch, vmem, *operands):
    return pl.pallas_call(
        kernel,
        out_shape=jax.ShapeDtypeStruct(shape, jnp.float32),
        in_specs=specs,
        out_specs=VMEM,
        scratch_shapes=scratch,
        compiler_params=pltpu.CompilerParams(vmem_limit_bytes=vmem * MIB),
    )(*operands)


def solve(mine, other, spread, prior, epochs, width):
    scratch = [
        pltpu.VMEM((width, HALF), jnp.float32),
        pltpu.VMEM((epochs * width, width), jnp.bfloat16),
        pltpu.VMEM((epochs * width, width), jnp.bfloat16),
        pltpu.VMEM((epochs, epochs, width), jnp.float32),
    ]
    return call(solve_kernel, (1, width), [VMEM] * 4, scratch, 24, mine, other, spread, prior)


def exchange(x, axis, groups=None):
    return lax.all_to_all(
        x, axis, split_axis=0, concat_axis=0, tiled=True, axis_index_groups=groups
    )


def shards(
    ray_basis, delays, ray_station, ray_count, station_var, decay_factor, mode_variance, prior_mean
):
    rays, width = ray_basis.shape[1:]
    stations = station_var.shape[0]
    epochs = lax.axis_size("tm")
    parts = lax.axis_size("sta")
    chips = parts // 2
    scratch = [
        pltpu.SMEM((1, 1), jnp.int32),
        pltpu.SMEM((stations,), jnp.float32),
        pltpu.VMEM((rays, width), jnp.bfloat16),
        pltpu.VMEM((1, rays), jnp.bfloat16),
        pltpu.VMEM((1, rays), jnp.int32),
        pltpu.VMEM((1, width), jnp.float32),
        pltpu.VMEM((rays, width), jnp.bfloat16),
        pltpu.SemaphoreType.DMA((6,)),
    ]
    share = call(
        ray_kernel,
        (parts * SLAB, 1, HALF),
        [HBM] * 6,
        scratch,
        16,
        ray_count,
        station_var,
        ray_basis,
        delays,
        ray_station,
        decay_factor,
    )
    summed = call(
        sum_kernel, (epochs * SLAB, 1, HALF), [VMEM], [], 4, exchange(share, "sta")
    )
    ours = call(
        copy_kernel, (chips, epochs * SLAB, HALF), [VMEM], [], 4, exchange(summed, "tm")
    )
    same_core = [[2 * j + c for j in range(chips)] for c in range(2)]
    ours = ours.reshape(chips * epochs * SLAB, HALF)
    mine = exchange(ours, "sta", same_core).reshape(chips, epochs * SLAB, HALF)
    other = lax.ppermute(mine, "sta", [(i, i + 1 - 2 * (i % 2)) for i in range(parts)])
    return solve(mine, other, mode_variance[None], prior_mean[None], epochs, width)


def solution(mesh):
    placed = (
        P("tm", "sta", None),
        P("tm", "sta"),
        P("tm", "sta"),
        P("tm", "sta"),
        P("sta"),
        P("tm", None),
        P(),
        P(),
    )
    return jax.shard_map(
        shards, mesh=mesh, in_specs=placed, out_specs=P("tm", None), check_vma=False
    )
```

```python
import jax
import jax.numpy as jnp
from jax import lax
from jax.experimental import pallas as pl
from jax.experimental.pallas import tpu as pltpu
from jax.sharding import PartitionSpec as P

HALF = 128
TILE = 8
SLAB = TILE + 1
TOLERANCE = 1e-5
MOST_STEPS = 4000


def ray_kernel(
    count_hbm,
    var_hbm,
    basis_hbm,
    delay_hbm,
    station_hbm,
    decay_hbm,
    out_ref,
    count_ref,
    var_ref,
    basis_ref,
    delay_ref,
    station_ref,
    decay_ref,
    weighted,
    arrived,
):
    rays = basis_ref.shape[0]
    stations = var_ref.shape[0]
    small = [
        pltpu.make_async_copy(source, target, arrived.at[k])
        for k, (source, target) in enumerate(
            (
                (station_hbm, station_ref),
                (var_hbm, var_ref),
                (count_hbm, count_ref),
                (delay_hbm, delay_ref),
                (decay_hbm, decay_ref),
            )
        )
    ]
    whole = pltpu.make_async_copy(basis_hbm.at[0], basis_ref, arrived.at[len(small)])
    for copy in small:
        copy.start()
    whole.start()
    shard = lax.axis_index("sta")
    for copy in small:
        copy.wait()
    local = station_ref[...] - shard * stations
    variance = jnp.ones(local.shape, jnp.float32)
    for k in range(stations):
        variance = jnp.where(local == k, var_ref[k], variance)
    slot = lax.broadcasted_iota(jnp.int32, local.shape, 1)
    weight = jnp.where(slot < count_ref[0, 0], 1.0 / variance, 0.0)
    whole.wait()
    for start in range(0, rays, HALF):
        rows = slice(start, start + HALF)
        column = jnp.broadcast_to(weight[:, rows], (HALF, HALF)).T
        for lane in (0, HALF):
            lanes = slice(lane, lane + HALF)
            block = basis_ref[rows, lanes].astype(jnp.float32)
            weighted[rows, lanes] = (block * column).astype(jnp.bfloat16)
    scaled = weighted[...]
    information = lax.dot_general(
        scaled, basis_ref[...], (((0,), (0,)), ((), ())), preferred_element_type=jnp.float32
    )
    drive = jnp.dot(delay_ref[...], scaled, preferred_element_type=jnp.float32)
    first = information[:HALF, :HALF]
    second = information[HALF:, HALF:]
    row = lax.broadcasted_iota(jnp.int32, (HALF, HALF), 0)
    col = lax.broadcasted_iota(jnp.int32, (HALF, HALF), 1)
    diagonal = jnp.sum(jnp.where(row == col, second, 0.0), axis=0, keepdims=True)
    triangles = jnp.where(col >= row, first, second)
    corner = information[:HALF, HALF:]
    own = jnp.where(shard == 0, decay_ref[...], 0.0)
    extras = [drive[:, :HALF], drive[:, HALF:], diagonal, own[:, :HALF], own[:, HALF:]]
    blank = jnp.zeros((1, HALF), jnp.float32)
    for j in range(HALF // TILE):
        extra = extras[j] if j < len(extras) else blank
        for c, block in ((0, triangles), (1, corner)):
            base = (2 * j + c) * SLAB
            out_ref[base : base + TILE, 0, :] = block[j * TILE : j * TILE + TILE, :]
            out_ref[base + TILE, :, :] = extra


def sum_kernel(parts_ref, out_ref):
    total = parts_ref[0:TILE, 0, :]
    extra = parts_ref[TILE, :, :]
    for k in range(1, parts_ref.shape[0] // SLAB):
        base = k * SLAB
        total = total + parts_ref[base : base + TILE, 0, :]
        extra = extra + parts_ref[base + TILE, :, :]
    for k in range(out_ref.shape[0] // SLAB):
        base = k * SLAB
        out_ref[base : base + TILE, 0, :] = total
        out_ref[base + TILE, :, :] = extra


def copy_kernel(rows_ref, out_ref):
    epochs = rows_ref.shape[0] // SLAB
    for k in range(epochs):
        tile = rows_ref[k * SLAB : k * SLAB + TILE, 0, :]
        extra = rows_ref[k * SLAB + TILE, :, :]
        for j in range(out_ref.shape[0]):
            out_ref[j, k * TILE : k * TILE + TILE, :] = tile
            out_ref[j, epochs * TILE + k : epochs * TILE + k + 1, :] = extra


def solve_kernel(
    mine_ref,
    other_ref,
    spread_ref,
    prior_ref,
    out_ref,
    packed,
    high,
    low,
    response,
):
    epochs, _, width = response.shape
    chips = mine_ref.shape[0]
    core = lax.rem(lax.axis_index("sta"), 2)
    epoch_here = lax.axis_index("tm")
    row = lax.broadcasted_iota(jnp.int32, (HALF, HALF), 0)
    col = lax.broadcasted_iota(jnp.int32, (HALF, HALF), 1)

    def unpack(e, carry):
        place = pl.multiple_of(e * TILE, TILE)
        for j in range(chips):
            ours = pl.multiple_of(core * HALF + j * TILE, TILE)
            theirs = pl.multiple_of((1 - core) * HALF + j * TILE, TILE)
            packed[pl.ds(ours, TILE), :] = mine_ref[j, pl.ds(place, TILE), :]
            packed[pl.ds(theirs, TILE), :] = other_ref[j, pl.ds(place, TILE), :]
        triangles = packed[:HALF, :]
        corner = packed[HALF:, :]
        turned = triangles.T
        on_diagonal = row == col
        own = jnp.sum(jnp.where(on_diagonal, triangles, 0.0), axis=0, keepdims=True)
        first = jnp.where(on_diagonal, 0.0, jnp.where(col > row, triangles, turned))
        second = jnp.where(on_diagonal, 0.0, jnp.where(col < row, triangles, turned))
        base = pl.multiple_of(e * width, width)
        for r, c, block in ((0, 0, first), (0, 1, corner), (1, 0, corner.T), (1, 1, second)):
            rows = pl.ds(base + r * HALF, HALF)
            lanes = slice(c * HALF, c * HALF + HALF)
            upper = block.astype(jnp.bfloat16)
            high[rows, lanes] = upper
            low[rows, lanes] = (block - upper.astype(jnp.float32)).astype(jnp.bfloat16)
        return jnp.where(epoch_rows == e, own, carry)

    epoch_rows = lax.broadcasted_iota(jnp.int32, (epochs, HALF), 0)
    corner_diagonal = lax.fori_loop(0, epochs, unpack, jnp.zeros((epochs, HALF), jnp.float32))

    def extra(k):
        return mine_ref[k, epochs * TILE : epochs * TILE + epochs, :]

    drive = jnp.concatenate([extra(0), extra(1)], axis=1)
    decay = jnp.concatenate([extra(3), extra(4)], axis=1)
    diagonal = jnp.concatenate([corner_diagonal, extra(2)], axis=1)
    inverse_noise = 1.0 / ((1.0 - decay * decay) * spread_ref[...])
    index = lax.broadcasted_iota(jnp.int32, (epochs, width), 0)
    pull = decay * inverse_noise
    link_back = jnp.where(index == 0, 0.0, pull)
    link = jnp.where(index == epochs - 1, 0.0, pltpu.roll(pull, epochs - 1, 0))
    carried = jnp.where(index == epochs - 1, 0.0, pltpu.roll(decay * pull, epochs - 1, 0))
    middle = inverse_noise + carried + diagonal
    right = drive + jnp.where(index == 0, pull * prior_ref[...], 0.0)

    at = lambda x, e: x[e : e + 1, :]
    ahead = [at(middle, 0)]
    up = []
    for e in range(epochs - 1):
        up.append(at(link, e) / ahead[e])
        ahead.append(at(middle, e + 1) - at(link, e) * up[e])
    behind = at(middle, epochs - 1)
    down = [None] * epochs
    centre = [None] * epochs
    centre[epochs - 1] = 1.0 / ahead[epochs - 1]
    for e in reversed(range(epochs - 1)):
        down[e] = at(link, e) / behind
        reduced = at(link, e) * down[e]
        behind = at(middle, e) - reduced
        centre[e] = 1.0 / (ahead[e] - reduced)
    below = jnp.zeros((epochs, width), jnp.float32)
    for e in range(epochs):
        if e:
            below = below * down[e - 1]
        below = jnp.where(index == e, centre[e], below)
        response[e] = below
    above = jnp.where(index == epochs - 1, centre[epochs - 1], 0.0)
    for e in reversed(range(epochs - 1)):
        above = above * up[e]
        response[e] = response[e] + above
        above = jnp.where(index == e, centre[e], above)

    def precondition(r):
        total = at(r, 0) * response[0]
        for e in range(1, epochs):
            total = total + at(r, e) * response[e]
        return total

    def apply(p):
        blocks = []
        for e in range(epochs):
            kept = jnp.where(index == e, p, 0.0)
            upper = kept.astype(jnp.bfloat16)
            rest = (kept - upper.astype(jnp.float32)).astype(jnp.bfloat16)
            blocks.append(jnp.concatenate([upper, rest], axis=0))
        left = jnp.concatenate(blocks, axis=1)
        by_high = jnp.dot(left, high[...], preferred_element_type=jnp.float32)
        by_low = jnp.dot(left[:epochs], low[...], preferred_element_type=jnp.float32)
        near = (
            middle * p
            - link * pltpu.roll(p, epochs - 1, 0)
            - link_back * pltpu.roll(p, 1, 0)
        )
        return near + (by_high[:epochs] + by_high[epochs:] + by_low)

    def inner(a, b):
        return jnp.sum(jnp.sum(a * b, axis=0, keepdims=True), axis=1, keepdims=True)

    start = precondition(right)
    size = inner(right, start)
    bound = size[0, 0] * (TOLERANCE * TOLERANCE)

    def unfinished(state):
        return jnp.logical_and(state[0] < MOST_STEPS, state[4][0, 0] > bound)

    def step(state):
        count, x, r, p, size = state
        image = apply(p)
        energy = inner(p, image)
        length = jnp.where(energy > 0.0, size / energy, 0.0)
        x = x + length * p
        r = r - length * image
        z = precondition(r)
        fresh = inner(r, z)
        ratio = jnp.where(size > 0.0, fresh / size, 0.0)
        p = z + ratio * p
        return (count + 1, x, r, p, fresh)

    zero = jnp.zeros((epochs, width), jnp.float32)
    solved = lax.while_loop(unfinished, step, (0, zero, right, start, size))[1]
    out_ref[...] = jnp.sum(jnp.where(index == epoch_here, solved, 0.0), axis=0, keepdims=True)


VMEM = pl.BlockSpec(memory_space=pltpu.VMEM)
HBM = pl.BlockSpec(memory_space=pltpu.HBM)
MIB = 2**20


def call(kernel, shape, specs, scratch, vmem, *operands):
    return pl.pallas_call(
        kernel,
        out_shape=jax.ShapeDtypeStruct(shape, jnp.float32),
        in_specs=specs,
        out_specs=VMEM,
        scratch_shapes=scratch,
        compiler_params=pltpu.CompilerParams(vmem_limit_bytes=vmem * MIB),
    )(*operands)


def solve(mine, other, spread, prior, epochs, width):
    scratch = [
        pltpu.VMEM((width, HALF), jnp.float32),
        pltpu.VMEM((epochs * width, width), jnp.bfloat16),
        pltpu.VMEM((epochs * width, width), jnp.bfloat16),
        pltpu.VMEM((epochs, epochs, width), jnp.float32),
    ]
    return call(solve_kernel, (1, width), [VMEM] * 4, scratch, 24, mine, other, spread, prior)


def exchange(x, axis, groups=None):
    return lax.all_to_all(
        x, axis, split_axis=0, concat_axis=0, tiled=True, axis_index_groups=groups
    )


def shards(
    ray_basis, delays, ray_station, ray_count, station_var, decay_factor, mode_variance, prior_mean
):
    rays, width = ray_basis.shape[1:]
    stations = station_var.shape[0]
    epochs = lax.axis_size("tm")
    parts = lax.axis_size("sta")
    chips = parts // 2
    scratch = [
        pltpu.SMEM((1, 1), jnp.int32),
        pltpu.SMEM((stations,), jnp.float32),
        pltpu.VMEM((rays, width), jnp.bfloat16),
        pltpu.VMEM((1, rays), jnp.bfloat16),
        pltpu.VMEM((1, rays), jnp.int32),
        pltpu.VMEM((1, width), jnp.float32),
        pltpu.VMEM((rays, width), jnp.bfloat16),
        pltpu.SemaphoreType.DMA((6,)),
    ]
    share = call(
        ray_kernel,
        (parts * SLAB, 1, HALF),
        [HBM] * 6,
        scratch,
        60,
        ray_count,
        station_var,
        ray_basis,
        delays,
        ray_station,
        decay_factor,
    )
    summed = call(
        sum_kernel, (epochs * SLAB, 1, HALF), [VMEM], [], 4, exchange(share, "sta")
    )
    ours = call(
        copy_kernel, (chips, epochs * SLAB, HALF), [VMEM], [], 4, exchange(summed, "tm")
    )
    same_core = [[2 * j + c for j in range(chips)] for c in range(2)]
    ours = ours.reshape(chips * epochs * SLAB, HALF)
    mine = exchange(ours, "sta", same_core).reshape(chips, epochs * SLAB, HALF)
    other = lax.ppermute(mine, "sta", [(i, i + 1 - 2 * (i % 2)) for i in range(parts)])
    return solve(mine, other, mode_variance[None], prior_mean[None], epochs, width)


def solution(mesh):
    placed = (
        P("tm", "sta", None),
        P("tm", "sta"),
        P("tm", "sta"),
        P("tm", "sta"),
        P("sta"),
        P("tm", None),
        P(),
        P(),
    )
    return jax.shard_map(
        shards, mesh=mesh, in_specs=placed, out_specs=P("tm", None), check_vma=False
    )
```

```python
import jax
import jax.numpy as jnp
from jax import lax
from jax.experimental import pallas as pl
from jax.experimental.pallas import tpu as pltpu
from jax.sharding import PartitionSpec as P

HALF = 128
TILE = 8
SLAB = TILE + 1
TOLERANCE = 1e-5
MOST_STEPS = 4000


def ray_kernel(
    count_hbm,
    var_hbm,
    basis_hbm,
    delay_hbm,
    station_hbm,
    decay_hbm,
    out_ref,
    count_ref,
    var_ref,
    basis_ref,
    delay_ref,
    station_ref,
    decay_ref,
    weighted,
    arrived,
):
    rays = basis_ref.shape[0]
    stations = var_ref.shape[0]
    small = [
        pltpu.make_async_copy(source, target, arrived.at[k])
        for k, (source, target) in enumerate(
            (
                (station_hbm, station_ref),
                (var_hbm, var_ref),
                (count_hbm, count_ref),
                (delay_hbm, delay_ref),
                (decay_hbm, decay_ref),
            )
        )
    ]
    whole = pltpu.make_async_copy(basis_hbm.at[0], basis_ref, arrived.at[len(small)])
    for copy in small:
        copy.start()
    whole.start()
    shard = lax.axis_index("sta")
    for copy in small:
        copy.wait()
    local = station_ref[...] - shard * stations
    variance = jnp.ones(local.shape, jnp.float32)
    for k in range(stations):
        variance = jnp.where(local == k, var_ref[k], variance)
    slot = lax.broadcasted_iota(jnp.int32, local.shape, 1)
    weight = jnp.where(slot < count_ref[0, 0], 1.0 / variance, 0.0)
    whole.wait()
    for start in range(0, rays, HALF):
        rows = slice(start, start + HALF)
        column = jnp.broadcast_to(weight[:, rows], (HALF, HALF)).T
        for lane in (0, HALF):
            lanes = slice(lane, lane + HALF)
            block = basis_ref[rows, lanes].astype(jnp.float32)
            weighted[rows, lanes] = (block * column).astype(jnp.bfloat16)
    scaled = weighted[...]
    information = lax.dot_general(
        scaled, basis_ref[...], (((0,), (0,)), ((), ())), preferred_element_type=jnp.float32
    )
    drive = jnp.dot(delay_ref[...], scaled, preferred_element_type=jnp.float32)
    first = information[:HALF, :HALF]
    second = information[HALF:, HALF:]
    row = lax.broadcasted_iota(jnp.int32, (HALF, HALF), 0)
    col = lax.broadcasted_iota(jnp.int32, (HALF, HALF), 1)
    diagonals = [
        jnp.sum(jnp.where(row == col, block, 0.0), axis=0, keepdims=True) for block in (first, second)
    ]
    triangles = jnp.where(col >= row, first, second)
    corner = information[:HALF, HALF:]
    own = jnp.where(shard == 0, decay_ref[...], 0.0)
    extras = [drive[:, :HALF], drive[:, HALF:], *diagonals, own[:, :HALF], own[:, HALF:]]
    blank = jnp.zeros((1, HALF), jnp.float32)
    for j in range(HALF // TILE):
        extra = extras[j] if j < len(extras) else blank
        for c, block in ((0, triangles), (1, corner)):
            base = (2 * j + c) * SLAB
            out_ref[base : base + TILE, 0, :] = block[j * TILE : j * TILE + TILE, :]
            out_ref[base + TILE, :, :] = extra


def sum_kernel(parts_ref, out_ref):
    total = parts_ref[0:TILE, 0, :]
    extra = parts_ref[TILE, :, :]
    for k in range(1, parts_ref.shape[0] // SLAB):
        base = k * SLAB
        total = total + parts_ref[base : base + TILE, 0, :]
        extra = extra + parts_ref[base + TILE, :, :]
    for k in range(out_ref.shape[0] // SLAB):
        base = k * SLAB
        out_ref[base : base + TILE, 0, :] = total
        out_ref[base + TILE, :, :] = extra


def copy_kernel(rows_ref, out_ref):
    epochs = rows_ref.shape[0] // SLAB
    for k in range(epochs):
        tile = rows_ref[k * SLAB : k * SLAB + TILE, 0, :]
        extra = rows_ref[k * SLAB + TILE, :, :]
        for j in range(out_ref.shape[0]):
            out_ref[j, k * TILE : k * TILE + TILE, :] = tile
            out_ref[j, epochs * TILE + k : epochs * TILE + k + 1, :] = extra


def unpack(slabs_ref, triangles, high, low, epochs, width):
    chips = slabs_ref.shape[0]
    row = lax.broadcasted_iota(jnp.int32, (HALF, HALF), 0)
    col = lax.broadcasted_iota(jnp.int32, (HALF, HALF), 1)

    def one(e, carry):
        place = pl.multiple_of(e * TILE, TILE)
        block = jnp.concatenate(
            [slabs_ref[j, pl.ds(place, TILE), :] for j in range(chips)], axis=0
        )
        turned = block.T
        pair = (block, turned)
        if triangles:
            pair = (
                jnp.where(row == col, 0.0, jnp.where(col > row, block, turned)),
                jnp.where(row == col, 0.0, jnp.where(col < row, block, turned)),
            )
        for r in range(2):
            rows = pl.ds(pl.multiple_of(e * width + r * HALF, HALF), HALF)
            lane = (r if triangles else 1 - r) * HALF
            upper = pair[r].astype(jnp.bfloat16)
            high[rows, lane : lane + HALF] = upper
            low[rows, lane : lane + HALF] = (pair[r] - upper.astype(jnp.float32)).astype(jnp.bfloat16)
        return carry

    lax.fori_loop(0, epochs, one, 0, unroll=4)


def prepare_kernel(mine_ref, spread_ref, prior_ref, high, low, response, system):
    epochs, _, width = response.shape
    core = lax.rem(lax.axis_index("sta"), 2)
    pl.when(core == 0)(lambda: unpack(mine_ref, True, high, low, epochs, width))
    pl.when(core == 1)(lambda: unpack(mine_ref, False, high, low, epochs, width))

    def extra(k):
        rows = slice(epochs * TILE, epochs * TILE + epochs)
        return jnp.concatenate([mine_ref[k, rows, :], mine_ref[k + 1, rows, :]], axis=1)

    drive, diagonal, decay = extra(0), extra(2), extra(4)
    inverse_noise = 1.0 / ((1.0 - decay * decay) * spread_ref[...])
    index = lax.broadcasted_iota(jnp.int32, (epochs, width), 0)
    pull = decay * inverse_noise
    link_back = jnp.where(index == 0, 0.0, pull)
    link = jnp.where(index == epochs - 1, 0.0, pltpu.roll(pull, epochs - 1, 0))
    carried = jnp.where(index == epochs - 1, 0.0, pltpu.roll(decay * pull, epochs - 1, 0))
    middle = inverse_noise + carried + diagonal
    right = drive + jnp.where(index == 0, pull * prior_ref[...], 0.0)
    system[0] = middle
    system[1] = link
    system[2] = link_back
    system[3] = right

    at = lambda x, e: x[e : e + 1, :]
    ahead = [at(middle, 0)]
    up = []
    for e in range(epochs - 1):
        up.append(at(link, e) / ahead[e])
        ahead.append(at(middle, e + 1) - at(link, e) * up[e])
    behind = at(middle, epochs - 1)
    down = [None] * epochs
    centre = [None] * epochs
    centre[epochs - 1] = 1.0 / ahead[epochs - 1]
    for e in reversed(range(epochs - 1)):
        down[e] = at(link, e) / behind
        reduced = at(link, e) * down[e]
        behind = at(middle, e) - reduced
        centre[e] = 1.0 / (ahead[e] - reduced)
    below = jnp.zeros((epochs, width), jnp.float32)
    for e in range(epochs):
        if e:
            below = below * down[e - 1]
        below = jnp.where(index == e, centre[e], below)
        response[e] = below
    above = jnp.where(index == epochs - 1, centre[epochs - 1], 0.0)
    for e in reversed(range(epochs - 1)):
        above = above * up[e]
        response[e] = response[e] + above
        above = jnp.where(index == e, centre[e], above)


def solve_kernel(other_ref, high_in, low_in, response, system, out_ref, high, low):
    epochs, _, width = response.shape
    core = lax.rem(lax.axis_index("sta"), 2)
    epoch_here = lax.axis_index("tm")
    pl.when(core == 0)(lambda: unpack(other_ref, False, high, low, epochs, width))
    pl.when(core == 1)(lambda: unpack(other_ref, True, high, low, epochs, width))
    middle, link, link_back, right = (system[k] for k in range(4))
    index = lax.broadcasted_iota(jnp.int32, (epochs, width), 0)
    at = lambda x, e: x[e : e + 1, :]

    def precondition(r):
        total = at(r, 0) * response[0]
        for e in range(1, epochs):
            total = total + at(r, e) * response[e]
        return total

    def apply(p):
        blocks = []
        for e in range(epochs):
            kept = jnp.where(index == e, p, 0.0)
            upper = kept.astype(jnp.bfloat16)
            rest = (kept - upper.astype(jnp.float32)).astype(jnp.bfloat16)
            blocks.append(jnp.concatenate([upper, rest], axis=0))
        left = jnp.concatenate(blocks, axis=1)
        by_high = jnp.dot(left, high[...], preferred_element_type=jnp.float32)
        by_low = jnp.dot(left[:epochs], low[...], preferred_element_type=jnp.float32)
        near = (
            middle * p
            - link * pltpu.roll(p, epochs - 1, 0)
            - link_back * pltpu.roll(p, 1, 0)
        )
        return near + (by_high[:epochs] + by_high[epochs:] + by_low)

    def inner(a, b):
        return jnp.sum(jnp.sum(a * b, axis=0, keepdims=True), axis=1, keepdims=True)

    start = precondition(right)
    size = inner(right, start)
    bound = size[0, 0] * (TOLERANCE * TOLERANCE)

    def unfinished(state):
        return jnp.logical_and(state[0] < MOST_STEPS, state[4][0, 0] > bound)

    def step(state):
        count, x, r, p, size = state
        image = apply(p)
        energy = inner(p, image)
        length = jnp.where(energy > 0.0, size / energy, 0.0)
        x = x + length * p
        r = r - length * image
        z = precondition(r)
        fresh = inner(r, z)
        ratio = jnp.where(size > 0.0, fresh / size, 0.0)
        p = z + ratio * p
        return (count + 1, x, r, p, fresh)

    zero = jnp.zeros((epochs, width), jnp.float32)
    solved = lax.while_loop(unfinished, step, (0, zero, right, start, size))[1]
    out_ref[...] = jnp.sum(jnp.where(index == epoch_here, solved, 0.0), axis=0, keepdims=True)


VMEM = pl.BlockSpec(memory_space=pltpu.VMEM)
HBM = pl.BlockSpec(memory_space=pltpu.HBM)
MIB = 2**20


def call(kernel, shape, specs, scratch, vmem, *operands):
    return pl.pallas_call(
        kernel,
        out_shape=pltpu.VMEM(shape, jnp.float32),
        in_specs=specs,
        out_specs=VMEM,
        scratch_shapes=scratch,
        compiler_params=pltpu.CompilerParams(vmem_limit_bytes=vmem * MIB),
    )(*operands)


def solve(mine, other, spread, prior, epochs, width):
    halves = [pltpu.VMEM((epochs * width, width), jnp.bfloat16)] * 2
    tables = [
        pltpu.VMEM((epochs, epochs, width), jnp.float32),
        pltpu.VMEM((4, epochs, width), jnp.float32),
    ]
    high, low, response, system = pl.pallas_call(
        prepare_kernel,
        out_shape=halves + tables,
        in_specs=[VMEM] * 3,
        out_specs=[VMEM] * 4,
        compiler_params=pltpu.CompilerParams(vmem_limit_bytes=8 * MIB),
        cost_estimate=pl.CostEstimate(flops=2**24, bytes_accessed=2**22, transcendentals=0),
    )(mine, spread, prior)
    return pl.pallas_call(
        solve_kernel,
        out_shape=[jax.ShapeDtypeStruct((1, width), jnp.float32)] + halves,
        in_specs=[VMEM] * 5,
        out_specs=[VMEM] * 3,
        input_output_aliases={1: 1, 2: 2},
        compiler_params=pltpu.CompilerParams(vmem_limit_bytes=8 * MIB),
    )(other, high, low, response, system)[0]


def exchange(x, axis, groups=None):
    return lax.all_to_all(
        x, axis, split_axis=0, concat_axis=0, tiled=True, axis_index_groups=groups
    )


def shards(
    ray_basis, delays, ray_station, ray_count, station_var, decay_factor, mode_variance, prior_mean
):
    rays, width = ray_basis.shape[1:]
    stations = station_var.shape[0]
    epochs = lax.axis_size("tm")
    parts = lax.axis_size("sta")
    chips = parts // 2
    scratch = [
        pltpu.SMEM((1, 1), jnp.int32),
        pltpu.SMEM((stations,), jnp.float32),
        pltpu.VMEM((rays, width), jnp.bfloat16),
        pltpu.VMEM((1, rays), jnp.bfloat16),
        pltpu.VMEM((1, rays), jnp.int32),
        pltpu.VMEM((1, width), jnp.float32),
        pltpu.VMEM((rays, width), jnp.bfloat16),
        pltpu.SemaphoreType.DMA((6,)),
    ]
    share = call(
        ray_kernel,
        (parts * SLAB, 1, HALF),
        [HBM] * 6,
        scratch,
        60,
        ray_count,
        station_var,
        ray_basis,
        delays,
        ray_station,
        decay_factor,
    )
    summed = call(
        sum_kernel, (epochs * SLAB, 1, HALF), [VMEM], [], 4, exchange(share, "sta")
    )
    ours = call(
        copy_kernel, (chips, epochs * SLAB, HALF), [VMEM], [], 4, exchange(summed, "tm")
    )
    same_core = [[2 * j + c for j in range(chips)] for c in range(2)]
    ours = ours.reshape(chips * epochs * SLAB, HALF)
    mine = exchange(ours, "sta", same_core).reshape(chips, epochs * SLAB, HALF)
    other = lax.ppermute(mine, "sta", [(i, i + 1 - 2 * (i % 2)) for i in range(parts)])
    return solve(mine, other, mode_variance[None], prior_mean[None], epochs, width)


def solution(mesh):
    placed = (
        P("tm", "sta", None),
        P("tm", "sta"),
        P("tm", "sta"),
        P("tm", "sta"),
        P("sta"),
        P("tm", None),
        P(),
        P(),
    )
    return jax.shard_map(
        shards, mesh=mesh, in_specs=placed, out_specs=P("tm", None), check_vma=False
    )
```

```python
import jax
import jax.numpy as jnp
from jax import lax
from jax.experimental import pallas as pl
from jax.experimental.pallas import tpu as pltpu
from jax.sharding import PartitionSpec as P

HALF = 128
TILE = 8
SLAB = TILE + 1
TOLERANCE = 2e-5
PIECES = 4
MOST_STEPS = 4000


def ray_kernel(
    count_hbm,
    var_hbm,
    basis_hbm,
    delay_hbm,
    station_hbm,
    decay_hbm,
    out_ref,
    count_ref,
    var_ref,
    basis_ref,
    delay_ref,
    station_ref,
    decay_ref,
    weighted,
    arrived,
):
    rays = basis_ref.shape[0]
    stations = var_ref.shape[0]
    small = [
        pltpu.make_async_copy(source, target, arrived.at[k])
        for k, (source, target) in enumerate(
            (
                (station_hbm, station_ref),
                (var_hbm, var_ref),
                (count_hbm, count_ref),
                (delay_hbm, delay_ref),
                (decay_hbm, decay_ref),
            )
        )
    ]
    large = [
        pltpu.make_async_copy(
            basis_hbm.at[0, pl.ds(k * rays // PIECES, rays // PIECES)],
            basis_ref.at[pl.ds(k * rays // PIECES, rays // PIECES)],
            arrived.at[len(small) + k],
        )
        for k in range(PIECES)
    ]
    for copy in small + large:
        copy.start()
    shard = lax.axis_index("sta")
    for copy in small:
        copy.wait()
    local = station_ref[...] - shard * stations
    variance = jnp.ones(local.shape, jnp.float32)
    for k in range(stations):
        variance = jnp.where(local == k, var_ref[k], variance)
    slot = lax.broadcasted_iota(jnp.int32, local.shape, 1)
    weight = jnp.where(slot < count_ref[0, 0], 1.0 / variance, 0.0)
    for start in range(0, rays, HALF):
        if start % (rays // PIECES) == 0:
            large[start * PIECES // rays].wait()
        rows = slice(start, start + HALF)
        column = jnp.broadcast_to(weight[:, rows], (HALF, HALF)).T
        for lane in (0, HALF):
            lanes = slice(lane, lane + HALF)
            block = basis_ref[rows, lanes].astype(jnp.float32)
            weighted[rows, lanes] = (block * column).astype(jnp.bfloat16)
    scaled = weighted[...]
    information = lax.dot_general(
        scaled, basis_ref[...], (((0,), (0,)), ((), ())), preferred_element_type=jnp.float32
    )
    drive = jnp.dot(delay_ref[...], scaled, preferred_element_type=jnp.float32)
    first = information[:HALF, :HALF]
    second = information[HALF:, HALF:]
    row = lax.broadcasted_iota(jnp.int32, (HALF, HALF), 0)
    col = lax.broadcasted_iota(jnp.int32, (HALF, HALF), 1)
    diagonals = [
        jnp.sum(jnp.where(row == col, block, 0.0), axis=0, keepdims=True) for block in (first, second)
    ]
    triangles = jnp.where(col >= row, first, second)
    corner = information[:HALF, HALF:]
    own = jnp.where(shard == 0, decay_ref[...], 0.0)
    extras = [drive[:, :HALF], drive[:, HALF:], *diagonals, own[:, :HALF], own[:, HALF:]]
    blank = jnp.zeros((1, HALF), jnp.float32)
    for j in range(HALF // TILE):
        extra = extras[j] if j < len(extras) else blank
        for c, block in ((0, triangles), (1, corner)):
            base = (2 * j + c) * SLAB
            out_ref[base : base + TILE, 0, :] = block[j * TILE : j * TILE + TILE, :]
            out_ref[base + TILE, :, :] = extra


def sum_kernel(parts_ref, out_ref):
    total = parts_ref[0:TILE, 0, :]
    extra = parts_ref[TILE, :, :]
    for k in range(1, parts_ref.shape[0] // SLAB):
        base = k * SLAB
        total = total + parts_ref[base : base + TILE, 0, :]
        extra = extra + parts_ref[base + TILE, :, :]
    for k in range(out_ref.shape[0] // SLAB):
        base = k * SLAB
        out_ref[base : base + TILE, 0, :] = total
        out_ref[base + TILE, :, :] = extra


def copy_kernel(rows_ref, out_ref):
    epochs = rows_ref.shape[0] // SLAB
    for k in range(epochs):
        tile = rows_ref[k * SLAB : k * SLAB + TILE, 0, :]
        extra = rows_ref[k * SLAB + TILE, :, :]
        for j in range(out_ref.shape[0]):
            out_ref[j, k * TILE : k * TILE + TILE, :] = tile
            out_ref[j, epochs * TILE + k : epochs * TILE + k + 1, :] = extra


def unpack(slabs_ref, triangles, high, low, epochs, width):
    chips = slabs_ref.shape[0]
    row = lax.broadcasted_iota(jnp.int32, (HALF, HALF), 0)
    col = lax.broadcasted_iota(jnp.int32, (HALF, HALF), 1)

    def one(e, carry):
        place = pl.multiple_of(e * TILE, TILE)
        block = jnp.concatenate(
            [slabs_ref[j, pl.ds(place, TILE), :] for j in range(chips)], axis=0
        )
        turned = block.T
        pair = (block, turned)
        if triangles:
            pair = (
                jnp.where(row == col, 0.0, jnp.where(col > row, block, turned)),
                jnp.where(row == col, 0.0, jnp.where(col < row, block, turned)),
            )
        for r in range(2):
            rows = pl.ds(pl.multiple_of(e * width + r * HALF, HALF), HALF)
            lane = (r if triangles else 1 - r) * HALF
            upper = pair[r].astype(jnp.bfloat16)
            high[rows, lane : lane + HALF] = upper
            low[rows, lane : lane + HALF] = (pair[r] - upper.astype(jnp.float32)).astype(jnp.bfloat16)
        return carry

    lax.fori_loop(0, epochs, one, 0, unroll=4)


def prepare_kernel(mine_ref, spread_ref, prior_ref, high, low, response, system):
    epochs, _, width = response.shape
    core = lax.rem(lax.axis_index("sta"), 2)
    pl.when(core == 0)(lambda: unpack(mine_ref, True, high, low, epochs, width))
    pl.when(core == 1)(lambda: unpack(mine_ref, False, high, low, epochs, width))

    def extra(k):
        rows = slice(epochs * TILE, epochs * TILE + epochs)
        return jnp.concatenate([mine_ref[k, rows, :], mine_ref[k + 1, rows, :]], axis=1)

    drive, diagonal, decay = extra(0), extra(2), extra(4)
    inverse_noise = 1.0 / ((1.0 - decay * decay) * spread_ref[...])
    index = lax.broadcasted_iota(jnp.int32, (epochs, width), 0)
    pull = decay * inverse_noise
    link_back = jnp.where(index == 0, 0.0, pull)
    link = jnp.where(index == epochs - 1, 0.0, pltpu.roll(pull, epochs - 1, 0))
    carried = jnp.where(index == epochs - 1, 0.0, pltpu.roll(decay * pull, epochs - 1, 0))
    middle = inverse_noise + carried + diagonal
    right = drive + jnp.where(index == 0, pull * prior_ref[...], 0.0)
    system[0] = middle
    system[1] = link
    system[2] = link_back
    system[3] = right

    at = lambda x, e: x[e : e + 1, :]
    ahead = [at(middle, 0)]
    up = []
    for e in range(epochs - 1):
        up.append(at(link, e) / ahead[e])
        ahead.append(at(middle, e + 1) - at(link, e) * up[e])
    behind = at(middle, epochs - 1)
    down = [None] * epochs
    centre = [None] * epochs
    centre[epochs - 1] = 1.0 / ahead[epochs - 1]
    for e in reversed(range(epochs - 1)):
        down[e] = at(link, e) / behind
        reduced = at(link, e) * down[e]
        behind = at(middle, e) - reduced
        centre[e] = 1.0 / (ahead[e] - reduced)
    below = jnp.zeros((epochs, width), jnp.float32)
    for e in range(epochs):
        if e:
            below = below * down[e - 1]
        below = jnp.where(index == e, centre[e], below)
        response[e] = below
    above = jnp.where(index == epochs - 1, centre[epochs - 1], 0.0)
    for e in reversed(range(epochs - 1)):
        above = above * up[e]
        response[e] = response[e] + above
        above = jnp.where(index == e, centre[e], above)


def solve_kernel(other_ref, high_in, low_in, response, system, out_ref, high, low):
    epochs, _, width = response.shape
    core = lax.rem(lax.axis_index("sta"), 2)
    epoch_here = lax.axis_index("tm")
    pl.when(core == 0)(lambda: unpack(other_ref, False, high, low, epochs, width))
    pl.when(core == 1)(lambda: unpack(other_ref, True, high, low, epochs, width))
    middle, link, link_back, right = (system[k] for k in range(4))
    index = lax.broadcasted_iota(jnp.int32, (epochs, width), 0)
    at = lambda x, e: x[e : e + 1, :]

    def precondition(r):
        total = at(r, 0) * response[0]
        for e in range(1, epochs):
            total = total + at(r, e) * response[e]
        return total

    def apply(p):
        blocks = []
        for e in range(epochs):
            kept = jnp.where(index == e, p, 0.0)
            upper = kept.astype(jnp.bfloat16)
            rest = (kept - upper.astype(jnp.float32)).astype(jnp.bfloat16)
            blocks.append(jnp.concatenate([upper, rest], axis=0))
        left = jnp.concatenate(blocks, axis=1)
        by_high = jnp.dot(left, high[...], preferred_element_type=jnp.float32)
        by_low = jnp.dot(left[:epochs], low[...], preferred_element_type=jnp.float32)
        near = (
            middle * p
            - link * pltpu.roll(p, epochs - 1, 0)
            - link_back * pltpu.roll(p, 1, 0)
        )
        return near + (by_high[:epochs] + by_high[epochs:] + by_low)

    def inner(a, b):
        return jnp.sum(jnp.sum(a * b, axis=0, keepdims=True), axis=1, keepdims=True)

    start = precondition(right)
    size = inner(right, start)
    bound = size[0, 0] * (TOLERANCE * TOLERANCE)

    def unfinished(state):
        return jnp.logical_and(state[0] < MOST_STEPS, state[1])

    def step(state):
        count, _, x, r, p, size = state
        again = size[0, 0] > bound
        image = apply(p)
        energy = inner(p, image)
        length = jnp.where(energy > 0.0, size / energy, 0.0)
        x = x + length * p
        r = r - length * image
        z = precondition(r)
        fresh = inner(r, z)
        ratio = jnp.where(size > 0.0, fresh / size, 0.0)
        p = z + ratio * p
        return (count + 1, again, x, r, p, fresh)

    zero = jnp.zeros((epochs, width), jnp.float32)
    solved = lax.while_loop(unfinished, step, (0, True, zero, right, start, size))[2]
    out_ref[...] = jnp.sum(jnp.where(index == epoch_here, solved, 0.0), axis=0, keepdims=True)


VMEM = pl.BlockSpec(memory_space=pltpu.VMEM)
HBM = pl.BlockSpec(memory_space=pltpu.HBM)
MIB = 2**20


def call(kernel, shape, specs, scratch, vmem, *operands):
    return pl.pallas_call(
        kernel,
        out_shape=pltpu.VMEM(shape, jnp.float32),
        in_specs=specs,
        out_specs=VMEM,
        scratch_shapes=scratch,
        compiler_params=pltpu.CompilerParams(vmem_limit_bytes=vmem * MIB),
    )(*operands)


def solve(mine, other, spread, prior, epochs, width):
    halves = [pltpu.VMEM((epochs * width, width), jnp.bfloat16)] * 2
    tables = [
        pltpu.VMEM((epochs, epochs, width), jnp.float32),
        pltpu.VMEM((4, epochs, width), jnp.float32),
    ]
    high, low, response, system = pl.pallas_call(
        prepare_kernel,
        out_shape=halves + tables,
        in_specs=[VMEM] * 3,
        out_specs=[VMEM] * 4,
        compiler_params=pltpu.CompilerParams(vmem_limit_bytes=8 * MIB),
        cost_estimate=pl.CostEstimate(flops=2**24, bytes_accessed=2**22, transcendentals=0),
    )(mine, spread, prior)
    return pl.pallas_call(
        solve_kernel,
        out_shape=[jax.ShapeDtypeStruct((1, width), jnp.float32)] + halves,
        in_specs=[VMEM] * 5,
        out_specs=[VMEM] * 3,
        input_output_aliases={1: 1, 2: 2},
        compiler_params=pltpu.CompilerParams(vmem_limit_bytes=8 * MIB),
    )(other, high, low, response, system)[0]


def exchange(x, axis, groups=None):
    return lax.all_to_all(
        x, axis, split_axis=0, concat_axis=0, tiled=True, axis_index_groups=groups
    )


def shards(
    ray_basis, delays, ray_station, ray_count, station_var, decay_factor, mode_variance, prior_mean
):
    rays, width = ray_basis.shape[1:]
    stations = station_var.shape[0]
    epochs = lax.axis_size("tm")
    parts = lax.axis_size("sta")
    chips = parts // 2
    scratch = [
        pltpu.SMEM((1, 1), jnp.int32),
        pltpu.SMEM((stations,), jnp.float32),
        pltpu.VMEM((rays, width), jnp.bfloat16),
        pltpu.VMEM((1, rays), jnp.bfloat16),
        pltpu.VMEM((1, rays), jnp.int32),
        pltpu.VMEM((1, width), jnp.float32),
        pltpu.VMEM((rays, width), jnp.bfloat16),
        pltpu.SemaphoreType.DMA((5 + PIECES,)),
    ]
    share = call(
        ray_kernel,
        (parts * SLAB, 1, HALF),
        [HBM] * 6,
        scratch,
        60,
        ray_count,
        station_var,
        ray_basis,
        delays,
        ray_station,
        decay_factor,
    )
    summed = call(
        sum_kernel, (epochs * SLAB, 1, HALF), [VMEM], [], 4, exchange(share, "sta")
    )
    ours = call(
        copy_kernel, (chips, epochs * SLAB, HALF), [VMEM], [], 4, exchange(summed, "tm")
    )
    same_core = [[2 * j + c for j in range(chips)] for c in range(2)]
    ours = ours.reshape(chips * epochs * SLAB, HALF)
    mine = exchange(ours, "sta", same_core).reshape(chips, epochs * SLAB, HALF)
    other = lax.ppermute(mine, "sta", [(i, i + 1 - 2 * (i % 2)) for i in range(parts)])
    return solve(mine, other, mode_variance[None], prior_mean[None], epochs, width)


def solution(mesh):
    placed = (
        P("tm", "sta", None),
        P("tm", "sta"),
        P("tm", "sta"),
        P("tm", "sta"),
        P("sta"),
        P("tm", None),
        P(),
        P(),
    )
    return jax.shard_map(
        shards, mesh=mesh, in_specs=placed, out_specs=P("tm", None), check_vma=False
    )
```

```python
import jax
import jax.numpy as jnp
from jax import lax
from jax.experimental import pallas as pl
from jax.experimental.pallas import tpu as pltpu
from jax.sharding import PartitionSpec as P

HALF = 128
TILE = 8
SLAB = TILE + 1
TOLERANCE = 2e-5
COARSE = 5e-2
SHORT_STEPS = 24
PIECES = 4
MOST_STEPS = 4000


def ray_kernel(
    count_hbm,
    var_hbm,
    basis_hbm,
    delay_hbm,
    station_hbm,
    decay_hbm,
    out_ref,
    count_ref,
    var_ref,
    basis_ref,
    delay_ref,
    station_ref,
    decay_ref,
    weighted,
    arrived,
):
    rays = basis_ref.shape[0]
    stations = var_ref.shape[0]
    small = [
        pltpu.make_async_copy(source, target, arrived.at[k])
        for k, (source, target) in enumerate(
            (
                (station_hbm, station_ref),
                (var_hbm, var_ref),
                (count_hbm, count_ref),
                (delay_hbm, delay_ref),
                (decay_hbm, decay_ref),
            )
        )
    ]
    large = [
        pltpu.make_async_copy(
            basis_hbm.at[0, pl.ds(k * rays // PIECES, rays // PIECES)],
            basis_ref.at[pl.ds(k * rays // PIECES, rays // PIECES)],
            arrived.at[len(small) + k],
        )
        for k in range(PIECES)
    ]
    for copy in small + large:
        copy.start()
    shard = lax.axis_index("sta")
    for copy in small:
        copy.wait()
    local = station_ref[...] - shard * stations
    variance = jnp.ones(local.shape, jnp.float32)
    for k in range(stations):
        variance = jnp.where(local == k, var_ref[k], variance)
    slot = lax.broadcasted_iota(jnp.int32, local.shape, 1)
    weight = jnp.where(slot < count_ref[0, 0], 1.0 / variance, 0.0)
    for start in range(0, rays, HALF):
        if start % (rays // PIECES) == 0:
            large[start * PIECES // rays].wait()
        rows = slice(start, start + HALF)
        column = jnp.broadcast_to(weight[:, rows], (HALF, HALF)).T
        for lane in (0, HALF):
            lanes = slice(lane, lane + HALF)
            block = basis_ref[rows, lanes].astype(jnp.float32)
            weighted[rows, lanes] = (block * column).astype(jnp.bfloat16)
    scaled = weighted[...]
    information = lax.dot_general(
        scaled, basis_ref[...], (((0,), (0,)), ((), ())), preferred_element_type=jnp.float32
    )
    drive = jnp.dot(delay_ref[...], scaled, preferred_element_type=jnp.float32)
    first = information[:HALF, :HALF]
    second = information[HALF:, HALF:]
    row = lax.broadcasted_iota(jnp.int32, (HALF, HALF), 0)
    col = lax.broadcasted_iota(jnp.int32, (HALF, HALF), 1)
    diagonals = [
        jnp.sum(jnp.where(row == col, block, 0.0), axis=0, keepdims=True) for block in (first, second)
    ]
    triangles = jnp.where(col >= row, first, second)
    corner = information[:HALF, HALF:]
    own = jnp.where(shard == 0, decay_ref[...], 0.0)
    extras = [drive[:, :HALF], drive[:, HALF:], *diagonals, own[:, :HALF], own[:, HALF:]]
    blank = jnp.zeros((1, HALF), jnp.float32)
    for j in range(HALF // TILE):
        extra = extras[j] if j < len(extras) else blank
        for c, block in ((0, triangles), (1, corner)):
            base = (2 * j + c) * SLAB
            out_ref[base : base + TILE, 0, :] = block[j * TILE : j * TILE + TILE, :]
            out_ref[base + TILE, :, :] = extra


def sum_kernel(parts_ref, out_ref):
    total = parts_ref[0:TILE, 0, :]
    extra = parts_ref[TILE, :, :]
    for k in range(1, parts_ref.shape[0] // SLAB):
        base = k * SLAB
        total = total + parts_ref[base : base + TILE, 0, :]
        extra = extra + parts_ref[base + TILE, :, :]
    for k in range(out_ref.shape[0] // SLAB):
        base = k * SLAB
        out_ref[base : base + TILE, 0, :] = total
        out_ref[base + TILE, :, :] = extra


def copy_kernel(rows_ref, out_ref):
    epochs = rows_ref.shape[0] // SLAB
    for k in range(epochs):
        tile = rows_ref[k * SLAB : k * SLAB + TILE, 0, :]
        extra = rows_ref[k * SLAB + TILE, :, :]
        for j in range(out_ref.shape[0]):
            out_ref[j, k * TILE : k * TILE + TILE, :] = tile
            out_ref[j, epochs * TILE + k : epochs * TILE + k + 1, :] = extra


def unpack(slabs_ref, triangles, high, low, epochs, width):
    chips = slabs_ref.shape[0]
    row = lax.broadcasted_iota(jnp.int32, (HALF, HALF), 0)
    col = lax.broadcasted_iota(jnp.int32, (HALF, HALF), 1)

    def one(e, carry):
        place = pl.multiple_of(e * TILE, TILE)
        block = jnp.concatenate(
            [slabs_ref[j, pl.ds(place, TILE), :] for j in range(chips)], axis=0
        )
        turned = block.T
        pair = (block, turned)
        if triangles:
            pair = (
                jnp.where(row == col, 0.0, jnp.where(col > row, block, turned)),
                jnp.where(row == col, 0.0, jnp.where(col < row, block, turned)),
            )
        for r in range(2):
            rows = pl.ds(pl.multiple_of(e * width + r * HALF, HALF), HALF)
            lane = (r if triangles else 1 - r) * HALF
            upper = pair[r].astype(jnp.bfloat16)
            high[rows, lane : lane + HALF] = upper
            low[rows, lane : lane + HALF] = (pair[r] - upper.astype(jnp.float32)).astype(jnp.bfloat16)
        return carry

    lax.fori_loop(0, epochs, one, 0, unroll=4)


def prepare_kernel(mine_ref, spread_ref, prior_ref, high, low, response, system):
    epochs, _, width = response.shape
    core = lax.rem(lax.axis_index("sta"), 2)
    pl.when(core == 0)(lambda: unpack(mine_ref, True, high, low, epochs, width))
    pl.when(core == 1)(lambda: unpack(mine_ref, False, high, low, epochs, width))

    def extra(k):
        rows = slice(epochs * TILE, epochs * TILE + epochs)
        return jnp.concatenate([mine_ref[k, rows, :], mine_ref[k + 1, rows, :]], axis=1)

    drive, diagonal, decay = extra(0), extra(2), extra(4)
    inverse_noise = 1.0 / ((1.0 - decay * decay) * spread_ref[...])
    index = lax.broadcasted_iota(jnp.int32, (epochs, width), 0)
    pull = decay * inverse_noise
    link_back = jnp.where(index == 0, 0.0, pull)
    link = jnp.where(index == epochs - 1, 0.0, pltpu.roll(pull, epochs - 1, 0))
    carried = jnp.where(index == epochs - 1, 0.0, pltpu.roll(decay * pull, epochs - 1, 0))
    middle = inverse_noise + carried + diagonal
    right = drive + jnp.where(index == 0, pull * prior_ref[...], 0.0)
    system[0] = middle
    system[1] = link
    system[2] = link_back
    system[3] = right

    at = lambda x, e: x[e : e + 1, :]
    ahead = [at(middle, 0)]
    up = []
    for e in range(epochs - 1):
        up.append(at(link, e) / ahead[e])
        ahead.append(at(middle, e + 1) - at(link, e) * up[e])
    behind = at(middle, epochs - 1)
    down = [None] * epochs
    centre = [None] * epochs
    centre[epochs - 1] = 1.0 / ahead[epochs - 1]
    for e in reversed(range(epochs - 1)):
        down[e] = at(link, e) / behind
        reduced = at(link, e) * down[e]
        behind = at(middle, e) - reduced
        centre[e] = 1.0 / (ahead[e] - reduced)
    below = jnp.zeros((epochs, width), jnp.float32)
    for e in range(epochs):
        if e:
            below = below * down[e - 1]
        below = jnp.where(index == e, centre[e], below)
        response[e] = below
    above = jnp.where(index == epochs - 1, centre[epochs - 1], 0.0)
    for e in reversed(range(epochs - 1)):
        above = above * up[e]
        response[e] = response[e] + above
        above = jnp.where(index == e, centre[e], above)


def solve_kernel(other_ref, high_in, low_in, response, system, out_ref, high, low):
    epochs, _, width = response.shape
    core = lax.rem(lax.axis_index("sta"), 2)
    epoch_here = lax.axis_index("tm")
    pl.when(core == 0)(lambda: unpack(other_ref, False, high, low, epochs, width))
    pl.when(core == 1)(lambda: unpack(other_ref, True, high, low, epochs, width))
    middle, link, link_back, right = (system[k] for k in range(4))
    index = lax.broadcasted_iota(jnp.int32, (epochs, width), 0)
    at = lambda x, e: x[e : e + 1, :]

    def precondition(r):
        total = at(r, 0) * response[0]
        for e in range(1, epochs):
            total = total + at(r, e) * response[e]
        return total

    def spread_rows(p):
        upper = p.astype(jnp.bfloat16).astype(jnp.float32)
        rest = p - upper
        which = lax.rem(lax.broadcasted_iota(jnp.int32, (2 * TILE, width), 0), TILE)
        lefts = []
        for g in range(0, epochs, TILE):
            both = jnp.concatenate([upper[g : g + TILE], rest[g : g + TILE]], axis=0)
            pieces = [jnp.where(which == e, both, 0.0).astype(jnp.bfloat16) for e in range(TILE)]
            lefts.append(jnp.concatenate(pieces, axis=1))
        return lefts

    def products(lefts, halves):
        groups = []
        for k, left in enumerate(lefts):
            rows = slice(k * TILE * width, (k + 1) * TILE * width)
            by = sum(jnp.dot(left, h[rows], preferred_element_type=jnp.float32) for h in halves)
            groups.append(by[:TILE] + by[TILE:])
        return jnp.concatenate(groups, axis=0)

    def apply(p, halves):
        near = (
            middle * p
            - link * pltpu.roll(p, epochs - 1, 0)
            - link_back * pltpu.roll(p, 1, 0)
        )
        return near + products(spread_rows(p), halves)

    def inner(a, b):
        return jnp.sum(jnp.sum(a * b, axis=0, keepdims=True), axis=1, keepdims=True)

    def iterate(halves, most, bound, x, r, p, size):
        def unfinished(state):
            return jnp.logical_and(state[0] < most, state[1] > 0)

        def step(state):
            count, _, x, r, p, size = state
            again = jnp.where(size[0, 0] > bound, 1, 0)
            image = apply(p, halves)
            energy = inner(p, image)
            length = jnp.where(energy > 0.0, size / energy, 0.0)
            x = x + length * p
            r = r - length * image
            z = precondition(r)
            fresh = inner(r, z)
            ratio = jnp.where(size > 0.0, fresh / size, 0.0)
            p = z + ratio * p
            return (count + 1, again, x, r, p, fresh)

        return lax.while_loop(unfinished, step, (0, 1, x, r, p, size))[2:]

    start = precondition(right)
    size = inner(right, start)
    bound = size[0, 0] * (TOLERANCE * TOLERANCE)
    zero = jnp.zeros((epochs, width), jnp.float32)
    coarse = size[0, 0] * (COARSE * COARSE)
    x, r, p, size = iterate((high, low), MOST_STEPS, coarse, zero, right, start, size)
    change, left_over, _, _ = iterate((high,), SHORT_STEPS, bound, zero, r, p, size)
    left_over = left_over - products(spread_rows(change), (low,))
    reached = inner(left_over, precondition(left_over))
    unsure = jnp.where(reached[0, 0] <= bound, 0, 1)

    def refine(state):
        _, solved = state
        better = reached < size
        r_now = jnp.where(better, left_over, r)
        z_now = precondition(r_now)
        solved = iterate(
            (high, low), MOST_STEPS, bound, solved, r_now, z_now, inner(r_now, z_now)
        )[0]
        return (0, solved)

    solved = jnp.where(reached < size, x + change, x)
    solved = lax.while_loop(lambda state: state[0] > 0, refine, (unsure, solved))[1]
    out_ref[...] = jnp.sum(jnp.where(index == epoch_here, solved, 0.0), axis=0, keepdims=True)


VMEM = pl.BlockSpec(memory_space=pltpu.VMEM)
HBM = pl.BlockSpec(memory_space=pltpu.HBM)
MIB = 2**20


def call(kernel, shape, specs, scratch, vmem, *operands):
    return pl.pallas_call(
        kernel,
        out_shape=pltpu.VMEM(shape, jnp.float32),
        in_specs=specs,
        out_specs=VMEM,
        scratch_shapes=scratch,
        compiler_params=pltpu.CompilerParams(vmem_limit_bytes=vmem * MIB),
    )(*operands)


def solve(mine, other, spread, prior, epochs, width):
    halves = [pltpu.VMEM((epochs * width, width), jnp.bfloat16)] * 2
    tables = [
        pltpu.VMEM((epochs, epochs, width), jnp.float32),
        pltpu.VMEM((4, epochs, width), jnp.float32),
    ]
    high, low, response, system = pl.pallas_call(
        prepare_kernel,
        out_shape=halves + tables,
        in_specs=[VMEM] * 3,
        out_specs=[VMEM] * 4,
        compiler_params=pltpu.CompilerParams(vmem_limit_bytes=8 * MIB),
        cost_estimate=pl.CostEstimate(flops=2**24, bytes_accessed=2**22, transcendentals=0),
    )(mine, spread, prior)
    return pl.pallas_call(
        solve_kernel,
        out_shape=[jax.ShapeDtypeStruct((1, width), jnp.float32)] + halves,
        in_specs=[VMEM] * 5,
        out_specs=[VMEM] * 3,
        input_output_aliases={1: 1, 2: 2},
        compiler_params=pltpu.CompilerParams(vmem_limit_bytes=8 * MIB),
    )(other, high, low, response, system)[0]


def exchange(x, axis, groups=None):
    return lax.all_to_all(
        x, axis, split_axis=0, concat_axis=0, tiled=True, axis_index_groups=groups
    )


def shards(
    ray_basis, delays, ray_station, ray_count, station_var, decay_factor, mode_variance, prior_mean
):
    rays, width = ray_basis.shape[1:]
    stations = station_var.shape[0]
    epochs = lax.axis_size("tm")
    parts = lax.axis_size("sta")
    chips = parts // 2
    scratch = [
        pltpu.SMEM((1, 1), jnp.int32),
        pltpu.SMEM((stations,), jnp.float32),
        pltpu.VMEM((rays, width), jnp.bfloat16),
        pltpu.VMEM((1, rays), jnp.bfloat16),
        pltpu.VMEM((1, rays), jnp.int32),
        pltpu.VMEM((1, width), jnp.float32),
        pltpu.VMEM((rays, width), jnp.bfloat16),
        pltpu.SemaphoreType.DMA((5 + PIECES,)),
    ]
    share = call(
        ray_kernel,
        (parts * SLAB, 1, HALF),
        [HBM] * 6,
        scratch,
        60,
        ray_count,
        station_var,
        ray_basis,
        delays,
        ray_station,
        decay_factor,
    )
    summed = call(
        sum_kernel, (epochs * SLAB, 1, HALF), [VMEM], [], 4, exchange(share, "sta")
    )
    ours = call(
        copy_kernel, (chips, epochs * SLAB, HALF), [VMEM], [], 4, exchange(summed, "tm")
    )
    same_core = [[2 * j + c for j in range(chips)] for c in range(2)]
    ours = ours.reshape(chips * epochs * SLAB, HALF)
    mine = exchange(ours, "sta", same_core).reshape(chips, epochs * SLAB, HALF)
    other = lax.ppermute(mine, "sta", [(i, i + 1 - 2 * (i % 2)) for i in range(parts)])
    return solve(mine, other, mode_variance[None], prior_mean[None], epochs, width)


def solution(mesh):
    placed = (
        P("tm", "sta", None),
        P("tm", "sta"),
        P("tm", "sta"),
        P("tm", "sta"),
        P("sta"),
        P("tm", None),
        P(),
        P(),
    )
    return jax.shard_map(
        shards, mesh=mesh, in_specs=placed, out_specs=P("tm", None), check_vma=False
    )
```

```python
import jax
import jax.numpy as jnp
from jax import lax
from jax.experimental import pallas as pl
from jax.experimental.pallas import tpu as pltpu
from jax.sharding import PartitionSpec as P

HALF = 128
TILE = 8
SLAB = TILE + 1
TOLERANCE = 2e-5
COARSE = 5e-2
SHORT_STEPS = 24
PIECES = 4
MOST_STEPS = 4000


def ray_kernel(
    count_hbm,
    var_hbm,
    basis_hbm,
    delay_hbm,
    station_hbm,
    decay_hbm,
    out_ref,
    count_ref,
    var_ref,
    basis_ref,
    delay_ref,
    station_ref,
    decay_ref,
    weighted,
    arrived,
):
    rays = basis_ref.shape[0]
    stations = var_ref.shape[0]
    small = [
        pltpu.make_async_copy(source, target, arrived.at[k])
        for k, (source, target) in enumerate(
            (
                (station_hbm, station_ref),
                (var_hbm, var_ref),
                (count_hbm, count_ref),
                (delay_hbm, delay_ref),
                (decay_hbm, decay_ref),
            )
        )
    ]
    large = [
        pltpu.make_async_copy(
            basis_hbm.at[0, pl.ds(k * rays // PIECES, rays // PIECES)],
            basis_ref.at[pl.ds(k * rays // PIECES, rays // PIECES)],
            arrived.at[len(small) + k],
        )
        for k in range(PIECES)
    ]
    for copy in small + large:
        copy.start()
    shard = lax.axis_index("sta")
    for copy in small:
        copy.wait()
    local = station_ref[...] - shard * stations
    variance = jnp.ones(local.shape, jnp.float32)
    for k in range(stations):
        variance = jnp.where(local == k, var_ref[k], variance)
    slot = lax.broadcasted_iota(jnp.int32, local.shape, 1)
    weight = jnp.where(slot < count_ref[0, 0], 1.0 / variance, 0.0)
    for start in range(0, rays, HALF):
        if start % (rays // PIECES) == 0:
            large[start * PIECES // rays].wait()
        rows = slice(start, start + HALF)
        column = jnp.broadcast_to(weight[:, rows], (HALF, HALF)).T
        for lane in (0, HALF):
            lanes = slice(lane, lane + HALF)
            block = basis_ref[rows, lanes].astype(jnp.float32)
            weighted[rows, lanes] = (block * column).astype(jnp.bfloat16)
    scaled = weighted[...]
    information = lax.dot_general(
        scaled, basis_ref[...], (((0,), (0,)), ((), ())), preferred_element_type=jnp.float32
    )
    drive = jnp.dot(delay_ref[...], scaled, preferred_element_type=jnp.float32)
    first = information[:HALF, :HALF]
    second = information[HALF:, HALF:]
    row = lax.broadcasted_iota(jnp.int32, (HALF, HALF), 0)
    col = lax.broadcasted_iota(jnp.int32, (HALF, HALF), 1)
    diagonals = [
        jnp.sum(jnp.where(row == col, block, 0.0), axis=0, keepdims=True) for block in (first, second)
    ]
    triangles = jnp.where(col >= row, first, second)
    corner = information[:HALF, HALF:]
    own = jnp.where(shard == 0, decay_ref[...], 0.0)
    extras = [drive[:, :HALF], drive[:, HALF:], *diagonals, own[:, :HALF], own[:, HALF:]]
    blank = jnp.zeros((1, HALF), jnp.float32)
    for j in range(HALF // TILE):
        extra = extras[j] if j < len(extras) else blank
        for c, block in ((0, triangles), (1, corner)):
            base = (2 * j + c) * SLAB
            out_ref[base : base + TILE, 0, :] = block[j * TILE : j * TILE + TILE, :]
            out_ref[base + TILE, :, :] = extra


def sum_kernel(parts_ref, out_ref):
    total = parts_ref[0:TILE, 0, :]
    extra = parts_ref[TILE, :, :]
    for k in range(1, parts_ref.shape[0] // SLAB):
        base = k * SLAB
        total = total + parts_ref[base : base + TILE, 0, :]
        extra = extra + parts_ref[base + TILE, :, :]
    for k in range(out_ref.shape[0] // SLAB):
        base = k * SLAB
        out_ref[base : base + TILE, 0, :] = total
        out_ref[base + TILE, :, :] = extra


def copy_kernel(rows_ref, out_ref):
    epochs = rows_ref.shape[0] // SLAB
    for k in range(epochs):
        tile = rows_ref[k * SLAB : k * SLAB + TILE, 0, :]
        extra = rows_ref[k * SLAB + TILE, :, :]
        for j in range(out_ref.shape[0]):
            out_ref[j, k * TILE : k * TILE + TILE, :] = tile
            out_ref[j, epochs * TILE + k : epochs * TILE + k + 1, :] = extra


def unpack(slabs_ref, triangles, high, low, epochs, width):
    chips = slabs_ref.shape[0]
    row = lax.broadcasted_iota(jnp.int32, (HALF, HALF), 0)
    col = lax.broadcasted_iota(jnp.int32, (HALF, HALF), 1)

    def one(e, carry):
        place = pl.multiple_of(e * TILE, TILE)
        block = jnp.concatenate(
            [slabs_ref[j, pl.ds(place, TILE), :] for j in range(chips)], axis=0
        )
        turned = block.T
        pair = (block, turned)
        if triangles:
            pair = (
                jnp.where(row == col, 0.0, jnp.where(col > row, block, turned)),
                jnp.where(row == col, 0.0, jnp.where(col < row, block, turned)),
            )
        for r in range(2):
            rows = pl.ds(pl.multiple_of(e * width + r * HALF, HALF), HALF)
            lane = (r if triangles else 1 - r) * HALF
            upper = pair[r].astype(jnp.bfloat16)
            high[rows, lane : lane + HALF] = upper
            low[rows, lane : lane + HALF] = (pair[r] - upper.astype(jnp.float32)).astype(jnp.bfloat16)
        return carry

    lax.fori_loop(0, epochs, one, 0, unroll=16)


def prepare_kernel(mine_ref, spread_ref, prior_ref, high, low, response, system):
    epochs, _, width = response.shape
    core = lax.rem(lax.axis_index("sta"), 2)
    pl.when(core == 0)(lambda: unpack(mine_ref, True, high, low, epochs, width))
    pl.when(core == 1)(lambda: unpack(mine_ref, False, high, low, epochs, width))

    def extra(k):
        rows = slice(epochs * TILE, epochs * TILE + epochs)
        return jnp.concatenate([mine_ref[k, rows, :], mine_ref[k + 1, rows, :]], axis=1)

    drive, diagonal, decay = extra(0), extra(2), extra(4)
    inverse_noise = 1.0 / ((1.0 - decay * decay) * spread_ref[...])
    index = lax.broadcasted_iota(jnp.int32, (epochs, width), 0)
    pull = decay * inverse_noise
    link_back = jnp.where(index == 0, 0.0, pull)
    link = jnp.where(index == epochs - 1, 0.0, pltpu.roll(pull, epochs - 1, 0))
    carried = jnp.where(index == epochs - 1, 0.0, pltpu.roll(decay * pull, epochs - 1, 0))
    middle = inverse_noise + carried + diagonal
    right = drive + jnp.where(index == 0, pull * prior_ref[...], 0.0)
    system[0] = middle
    system[1] = link
    system[2] = link_back
    system[3] = right

    at = lambda x, e: x[e : e + 1, :]
    ahead = [at(middle, 0)]
    up = []
    for e in range(epochs - 1):
        up.append(at(link, e) / ahead[e])
        ahead.append(at(middle, e + 1) - at(link, e) * up[e])
    behind = at(middle, epochs - 1)
    down = [None] * epochs
    centre = [None] * epochs
    centre[epochs - 1] = 1.0 / ahead[epochs - 1]
    for e in reversed(range(epochs - 1)):
        down[e] = at(link, e) / behind
        reduced = at(link, e) * down[e]
        behind = at(middle, e) - reduced
        centre[e] = 1.0 / (ahead[e] - reduced)
    below = jnp.zeros((epochs, width), jnp.float32)
    for e in range(epochs):
        if e:
            below = below * down[e - 1]
        below = jnp.where(index == e, centre[e], below)
        response[e] = below
    above = jnp.where(index == epochs - 1, centre[epochs - 1], 0.0)
    for e in reversed(range(epochs - 1)):
        above = above * up[e]
        response[e] = response[e] + above
        above = jnp.where(index == e, centre[e], above)


def solve_kernel(other_ref, high_in, low_in, response, system, out_ref, high, low):
    epochs, _, width = response.shape
    core = lax.rem(lax.axis_index("sta"), 2)
    epoch_here = lax.axis_index("tm")
    pl.when(core == 0)(lambda: unpack(other_ref, False, high, low, epochs, width))
    pl.when(core == 1)(lambda: unpack(other_ref, True, high, low, epochs, width))
    middle, link, link_back, right = (system[k] for k in range(4))
    index = lax.broadcasted_iota(jnp.int32, (epochs, width), 0)
    at = lambda x, e: x[e : e + 1, :]

    def precondition(r):
        total = at(r, 0) * response[0]
        for e in range(1, epochs):
            total = total + at(r, e) * response[e]
        return total

    def spread_rows(p):
        upper = p.astype(jnp.bfloat16).astype(jnp.float32)
        rest = p - upper
        which = lax.rem(lax.broadcasted_iota(jnp.int32, (2 * TILE, width), 0), TILE)
        lefts = []
        for g in range(0, epochs, TILE):
            both = jnp.concatenate([upper[g : g + TILE], rest[g : g + TILE]], axis=0)
            pieces = [jnp.where(which == e, both, 0.0).astype(jnp.bfloat16) for e in range(TILE)]
            lefts.append(jnp.concatenate(pieces, axis=1))
        return lefts

    def products(lefts, halves):
        groups = []
        for k, left in enumerate(lefts):
            rows = slice(k * TILE * width, (k + 1) * TILE * width)
            by = sum(jnp.dot(left, h[rows], preferred_element_type=jnp.float32) for h in halves)
            groups.append(by[:TILE] + by[TILE:])
        return jnp.concatenate(groups, axis=0)

    def apply(p, halves):
        near = (
            middle * p
            - link * pltpu.roll(p, epochs - 1, 0)
            - link_back * pltpu.roll(p, 1, 0)
        )
        return near + products(spread_rows(p), halves)

    def inner(a, b):
        return jnp.sum(jnp.sum(a * b, axis=0, keepdims=True), axis=1, keepdims=True)

    zero = jnp.zeros((epochs, width), jnp.float32)
    none = jnp.zeros((1, 1), jnp.float32)

    def iterate(halves, most, bound, x, r, z, p, path, before, length):
        def unfinished(state):
            return jnp.logical_and(state[0] < most, state[1] > 0)

        def step(state):
            count, _, x, r, z, p, path, before, length = state
            size = inner(r, z)
            again = jnp.where(size[0, 0] > bound, 1, 0)
            image = apply(z, halves)
            ratio = jnp.where(before > 0.0, size / before, 0.0)
            past = jnp.where(length > 0.0, ratio * size / length, 0.0)
            energy = inner(z, image) - past
            length = jnp.where(energy > 0.0, size / energy, 0.0)
            p = z + ratio * p
            path = image + ratio * path
            x = x + length * p
            r = r - length * path
            z = precondition(r)
            return (count + 1, again, x, r, z, p, path, size, length)

        return lax.while_loop(unfinished, step, (0, 1, x, r, z, p, path, before, length))[2:]

    start = precondition(right)
    size = inner(right, start)[0, 0]
    bound = size * (TOLERANCE * TOLERANCE)
    coarse = size * (COARSE * COARSE)
    x, r, z, *rest = iterate(
        (high, low), MOST_STEPS, coarse, zero, right, start, zero, zero, none, none
    )
    size = inner(r, z)
    change, left_over, *_ = iterate((high,), SHORT_STEPS, bound, zero, r, z, *rest)
    left_over = left_over - products(spread_rows(change), (low,))
    reached = inner(left_over, precondition(left_over))
    unsure = jnp.where(reached[0, 0] <= bound, 0, 1)

    def refine(state):
        better = reached < size
        r_now = jnp.where(better, left_over, r)
        solved = iterate(
            (high, low),
            MOST_STEPS,
            bound,
            state[1],
            r_now,
            precondition(r_now),
            zero,
            zero,
            none,
            none,
        )[0]
        return (0, solved)

    solved = jnp.where(reached < size, x + change, x)
    solved = lax.while_loop(lambda state: state[0] > 0, refine, (unsure, solved))[1]
    out_ref[...] = jnp.sum(jnp.where(index == epoch_here, solved, 0.0), axis=0, keepdims=True)


VMEM = pl.BlockSpec(memory_space=pltpu.VMEM)
HBM = pl.BlockSpec(memory_space=pltpu.HBM)
MIB = 2**20


def call(kernel, shape, specs, scratch, vmem, *operands):
    return pl.pallas_call(
        kernel,
        out_shape=pltpu.VMEM(shape, jnp.float32),
        in_specs=specs,
        out_specs=VMEM,
        scratch_shapes=scratch,
        compiler_params=pltpu.CompilerParams(vmem_limit_bytes=vmem * MIB),
    )(*operands)


def solve(mine, other, spread, prior, epochs, width):
    halves = [pltpu.VMEM((epochs * width, width), jnp.bfloat16)] * 2
    tables = [
        pltpu.VMEM((epochs, epochs, width), jnp.float32),
        pltpu.VMEM((4, epochs, width), jnp.float32),
    ]
    high, low, response, system = pl.pallas_call(
        prepare_kernel,
        out_shape=halves + tables,
        in_specs=[VMEM] * 3,
        out_specs=[VMEM] * 4,
        compiler_params=pltpu.CompilerParams(vmem_limit_bytes=8 * MIB),
        cost_estimate=pl.CostEstimate(flops=2**24, bytes_accessed=2**22, transcendentals=0),
    )(mine, spread, prior)
    return pl.pallas_call(
        solve_kernel,
        out_shape=[jax.ShapeDtypeStruct((1, width), jnp.float32)] + halves,
        in_specs=[VMEM] * 5,
        out_specs=[VMEM] * 3,
        input_output_aliases={1: 1, 2: 2},
        compiler_params=pltpu.CompilerParams(vmem_limit_bytes=8 * MIB),
    )(other, high, low, response, system)[0]


def exchange(x, axis, groups=None):
    return lax.all_to_all(
        x, axis, split_axis=0, concat_axis=0, tiled=True, axis_index_groups=groups
    )


def shards(
    ray_basis, delays, ray_station, ray_count, station_var, decay_factor, mode_variance, prior_mean
):
    rays, width = ray_basis.shape[1:]
    stations = station_var.shape[0]
    epochs = lax.axis_size("tm")
    parts = lax.axis_size("sta")
    chips = parts // 2
    scratch = [
        pltpu.SMEM((1, 1), jnp.int32),
        pltpu.SMEM((stations,), jnp.float32),
        pltpu.VMEM((rays, width), jnp.bfloat16),
        pltpu.VMEM((1, rays), jnp.bfloat16),
        pltpu.VMEM((1, rays), jnp.int32),
        pltpu.VMEM((1, width), jnp.float32),
        pltpu.VMEM((rays, width), jnp.bfloat16),
        pltpu.SemaphoreType.DMA((5 + PIECES,)),
    ]
    share = call(
        ray_kernel,
        (parts * SLAB, 1, HALF),
        [HBM] * 6,
        scratch,
        60,
        ray_count,
        station_var,
        ray_basis,
        delays,
        ray_station,
        decay_factor,
    )
    summed = call(
        sum_kernel, (epochs * SLAB, 1, HALF), [VMEM], [], 4, exchange(share, "sta")
    )
    ours = call(
        copy_kernel, (chips, epochs * SLAB, HALF), [VMEM], [], 4, exchange(summed, "tm")
    )
    same_core = [[2 * j + c for j in range(chips)] for c in range(2)]
    ours = ours.reshape(chips * epochs * SLAB, HALF)
    mine = exchange(ours, "sta", same_core).reshape(chips, epochs * SLAB, HALF)
    other = lax.ppermute(mine, "sta", [(i, i + 1 - 2 * (i % 2)) for i in range(parts)])
    return solve(mine, other, mode_variance[None], prior_mean[None], epochs, width)


def solution(mesh):
    placed = (
        P("tm", "sta", None),
        P("tm", "sta"),
        P("tm", "sta"),
        P("tm", "sta"),
        P("sta"),
        P("tm", None),
        P(),
        P(),
    )
    return jax.shard_map(
        shards, mesh=mesh, in_specs=placed, out_specs=P("tm", None), check_vma=False
    )
```

```python
import jax
import jax.numpy as jnp
from jax import lax
from jax.experimental import pallas as pl
from jax.experimental.pallas import tpu as pltpu
from jax.sharding import PartitionSpec as P

HALF = 128
TILE = 8
SLAB = TILE + 1
TOLERANCE = 2e-5
COARSE = 5e-2
SHORT_STEPS = 24
STEEP = 16.0
ROUNDS = 3
REDUCTION = 1e-4
PIECES = 4
MOST_STEPS = 1000


def ray_kernel(
    count_hbm,
    var_hbm,
    basis_hbm,
    delay_hbm,
    station_hbm,
    decay_hbm,
    out_ref,
    count_ref,
    var_ref,
    basis_ref,
    delay_ref,
    station_ref,
    decay_ref,
    weighted,
    arrived,
):
    rays = basis_ref.shape[0]
    stations = var_ref.shape[0]
    small = [
        pltpu.make_async_copy(source, target, arrived.at[k])
        for k, (source, target) in enumerate(
            (
                (station_hbm, station_ref),
                (var_hbm, var_ref),
                (count_hbm, count_ref),
                (delay_hbm, delay_ref),
                (decay_hbm, decay_ref),
            )
        )
    ]
    large = [
        pltpu.make_async_copy(
            basis_hbm.at[0, pl.ds(k * rays // PIECES, rays // PIECES)],
            basis_ref.at[pl.ds(k * rays // PIECES, rays // PIECES)],
            arrived.at[len(small) + k],
        )
        for k in range(PIECES)
    ]
    for copy in small + large:
        copy.start()
    shard = lax.axis_index("sta")
    for copy in small:
        copy.wait()
    local = station_ref[...] - shard * stations
    variance = jnp.ones(local.shape, jnp.float32)
    for k in range(stations):
        variance = jnp.where(local == k, var_ref[k], variance)
    slot = lax.broadcasted_iota(jnp.int32, local.shape, 1)
    weight = jnp.where(slot < count_ref[0, 0], 1.0 / variance, 0.0)
    for start in range(0, rays, HALF):
        if start % (rays // PIECES) == 0:
            large[start * PIECES // rays].wait()
        rows = slice(start, start + HALF)
        column = jnp.broadcast_to(weight[:, rows], (HALF, HALF)).T
        for lane in (0, HALF):
            lanes = slice(lane, lane + HALF)
            block = basis_ref[rows, lanes].astype(jnp.float32)
            weighted[rows, lanes] = (block * column).astype(jnp.bfloat16)
    scaled = weighted[...]
    information = lax.dot_general(
        scaled, basis_ref[...], (((0,), (0,)), ((), ())), preferred_element_type=jnp.float32
    )
    drive = jnp.dot(delay_ref[...], scaled, preferred_element_type=jnp.float32)
    first = information[:HALF, :HALF]
    second = information[HALF:, HALF:]
    row = lax.broadcasted_iota(jnp.int32, (HALF, HALF), 0)
    col = lax.broadcasted_iota(jnp.int32, (HALF, HALF), 1)
    diagonals = [
        jnp.sum(jnp.where(row == col, block, 0.0), axis=0, keepdims=True) for block in (first, second)
    ]
    triangles = jnp.where(col >= row, first, second)
    corner = information[:HALF, HALF:]
    own = jnp.where(shard == 0, decay_ref[...], 0.0)
    extras = [drive[:, :HALF], drive[:, HALF:], *diagonals, own[:, :HALF], own[:, HALF:]]
    blank = jnp.zeros((1, HALF), jnp.float32)
    for j in range(HALF // TILE):
        extra = extras[j] if j < len(extras) else blank
        for c, block in ((0, triangles), (1, corner)):
            base = (2 * j + c) * SLAB
            out_ref[base : base + TILE, 0, :] = block[j * TILE : j * TILE + TILE, :]
            out_ref[base + TILE, :, :] = extra


def sum_kernel(parts_ref, out_ref):
    total = parts_ref[0:TILE, 0, :]
    extra = parts_ref[TILE, :, :]
    for k in range(1, parts_ref.shape[0] // SLAB):
        base = k * SLAB
        total = total + parts_ref[base : base + TILE, 0, :]
        extra = extra + parts_ref[base + TILE, :, :]
    for k in range(out_ref.shape[0] // SLAB):
        base = k * SLAB
        out_ref[base : base + TILE, 0, :] = total
        out_ref[base + TILE, :, :] = extra


def copy_kernel(rows_ref, out_ref):
    epochs = rows_ref.shape[0] // SLAB
    for k in range(epochs):
        tile = rows_ref[k * SLAB : k * SLAB + TILE, 0, :]
        extra = rows_ref[k * SLAB + TILE, :, :]
        for j in range(out_ref.shape[0]):
            out_ref[j, k * TILE : k * TILE + TILE, :] = tile
            out_ref[j, epochs * TILE + k : epochs * TILE + k + 1, :] = extra


def whole(slabs_ref, e):
    place = pl.multiple_of(e * TILE, TILE)
    chips = slabs_ref.shape[0]
    return jnp.concatenate([slabs_ref[j, pl.ds(place, TILE), :] for j in range(chips)], axis=0)


def diagonal_blocks(triangles):
    row = lax.broadcasted_iota(jnp.int32, (HALF, HALF), 0)
    col = lax.broadcasted_iota(jnp.int32, (HALF, HALF), 1)
    turned = triangles.T
    return (
        jnp.where(row == col, 0.0, jnp.where(col > row, triangles, turned)),
        jnp.where(row == col, 0.0, jnp.where(col < row, triangles, turned)),
    )


def unpack(slabs_ref, triangles, high, low, epochs, width):
    def one(e, carry):
        block = whole(slabs_ref, e)
        pair = diagonal_blocks(block) if triangles else (block, block.T)
        for r in range(2):
            rows = pl.ds(pl.multiple_of(e * width + r * HALF, HALF), HALF)
            lane = (r if triangles else 1 - r) * HALF
            upper = pair[r].astype(jnp.bfloat16)
            high[rows, lane : lane + HALF] = upper
            low[rows, lane : lane + HALF] = (pair[r] - upper.astype(jnp.float32)).astype(jnp.bfloat16)
        return carry

    lax.fori_loop(0, epochs, one, 0, unroll=16)


def prepare_kernel(mine_ref, spread_ref, prior_ref, high, low, response, system):
    epochs, _, width = response.shape
    core = lax.rem(lax.axis_index("sta"), 2)
    pl.when(core == 0)(lambda: unpack(mine_ref, True, high, low, epochs, width))
    pl.when(core == 1)(lambda: unpack(mine_ref, False, high, low, epochs, width))

    def extra(k):
        rows = slice(epochs * TILE, epochs * TILE + epochs)
        return jnp.concatenate([mine_ref[k, rows, :], mine_ref[k + 1, rows, :]], axis=1)

    drive, diagonal, decay = extra(0), extra(2), extra(4)
    inverse_noise = 1.0 / ((1.0 - decay * decay) * spread_ref[...])
    index = lax.broadcasted_iota(jnp.int32, (epochs, width), 0)
    pull = decay * inverse_noise
    link_back = jnp.where(index == 0, 0.0, pull)
    link = jnp.where(index == epochs - 1, 0.0, pltpu.roll(pull, epochs - 1, 0))
    carried = jnp.where(index == epochs - 1, 0.0, pltpu.roll(decay * pull, epochs - 1, 0))
    middle = inverse_noise + carried + diagonal
    right = drive + jnp.where(index == 0, pull * prior_ref[...], 0.0)
    system[0] = middle
    system[1] = link
    system[2] = link_back
    system[3] = right
    system[4] = diagonal * spread_ref[...]

    at = lambda x, e: x[e : e + 1, :]
    ahead = [at(middle, 0)]
    up = []
    for e in range(epochs - 1):
        up.append(at(link, e) / ahead[e])
        ahead.append(at(middle, e + 1) - at(link, e) * up[e])
    behind = at(middle, epochs - 1)
    down = [None] * epochs
    centre = [None] * epochs
    centre[epochs - 1] = 1.0 / ahead[epochs - 1]
    for e in reversed(range(epochs - 1)):
        down[e] = at(link, e) / behind
        reduced = at(link, e) * down[e]
        behind = at(middle, e) - reduced
        centre[e] = 1.0 / (ahead[e] - reduced)
    below = jnp.zeros((epochs, width), jnp.float32)
    for e in range(epochs):
        if e:
            below = below * down[e - 1]
        below = jnp.where(index == e, centre[e], below)
        response[e] = below
    above = jnp.where(index == epochs - 1, centre[epochs - 1], 0.0)
    for e in reversed(range(epochs - 1)):
        above = above * up[e]
        response[e] = response[e] + above
        above = jnp.where(index == e, centre[e], above)


def solve_kernel(mine_ref, other_ref, high_in, low_in, response, system, out_ref, high, low):
    epochs, _, width = response.shape
    core = lax.rem(lax.axis_index("sta"), 2)
    epoch_here = lax.axis_index("tm")
    pl.when(core == 0)(lambda: unpack(other_ref, False, high, low, epochs, width))
    pl.when(core == 1)(lambda: unpack(other_ref, True, high, low, epochs, width))
    middle, link, link_back, right = (system[k] for k in range(4))
    index = lax.broadcasted_iota(jnp.int32, (epochs, width), 0)
    at = lambda x, e: x[e : e + 1, :]

    def precondition(r):
        total = at(r, 0) * response[0]
        for e in range(1, epochs):
            total = total + at(r, e) * response[e]
        return total

    def spread_rows(p):
        upper = p.astype(jnp.bfloat16).astype(jnp.float32)
        rest = p - upper
        which = lax.rem(lax.broadcasted_iota(jnp.int32, (2 * TILE, width), 0), TILE)
        lefts = []
        for g in range(0, epochs, TILE):
            both = jnp.concatenate([upper[g : g + TILE], rest[g : g + TILE]], axis=0)
            pieces = [jnp.where(which == e, both, 0.0).astype(jnp.bfloat16) for e in range(TILE)]
            lefts.append(jnp.concatenate(pieces, axis=1))
        return lefts

    def products(lefts, halves):
        groups = []
        for k, left in enumerate(lefts):
            rows = slice(k * TILE * width, (k + 1) * TILE * width)
            by = sum(jnp.dot(left, h[rows], preferred_element_type=jnp.float32) for h in halves)
            groups.append(by[:TILE] + by[TILE:])
        return jnp.concatenate(groups, axis=0)

    def near(p):
        return (
            middle * p
            - link * pltpu.roll(p, epochs - 1, 0)
            - link_back * pltpu.roll(p, 1, 0)
        )

    def apply(p, halves):
        return near(p) + products(spread_rows(p), halves)

    def residual(x):
        def one(e, total):
            mine = whole(mine_ref, e)
            other = whole(other_ref, e)
            corner = jnp.where(core == 0, other, mine)
            first, second = diagonal_blocks(jnp.where(core == 0, mine, other))
            kept = jnp.where(index == e, x, 0.0)
            left, right_half = kept[:, :HALF], kept[:, HALF:]
            dot = lambda u, m: jnp.dot(
                u, m, precision=lax.Precision.HIGHEST, preferred_element_type=jnp.float32
            )
            lower = dot(left, first) + dot(right_half, corner.T)
            upper = dot(left, corner) + dot(right_half, second)
            return total + jnp.concatenate([lower, upper], axis=1)

        return right - near(x) - lax.fori_loop(0, epochs, one, zero)

    def inner(a, b):
        return jnp.sum(jnp.sum(a * b, axis=0, keepdims=True), axis=1, keepdims=True)

    zero = jnp.zeros((epochs, width), jnp.float32)
    none = jnp.zeros((1, 1), jnp.float32)

    def iterate(halves, most, bound, x, r, z, p, path, before, length):
        def unfinished(state):
            return jnp.logical_and(state[0] < most, state[1] > 0)

        def step(state):
            count, _, x, r, z, p, path, before, length = state
            size = inner(r, z)
            again = jnp.where(size[0, 0] > bound, 1, 0)
            image = apply(z, halves)
            ratio = jnp.where(before > 0.0, size / before, 0.0)
            past = jnp.where(length > 0.0, ratio * size / length, 0.0)
            energy = inner(z, image) - past
            length = jnp.where(energy > 0.0, size / energy, 0.0)
            p = z + ratio * p
            path = image + ratio * path
            x = x + length * p
            r = r - length * path
            z = precondition(r)
            return (count + 1, again, x, r, z, p, path, size, length)

        return lax.while_loop(unfinished, step, (0, 1, x, r, z, p, path, before, length))[2:]

    start = precondition(right)
    size = inner(right, start)[0, 0]
    bound = size * (TOLERANCE * TOLERANCE)
    coarse = size * (COARSE * COARSE)
    x, r, z, *rest = iterate(
        (high, low), MOST_STEPS, coarse, zero, right, start, zero, zero, none, none
    )
    size = inner(r, z)
    change, left_over, *_ = iterate((high,), SHORT_STEPS, bound, zero, r, z, *rest)
    left_over = left_over - products(spread_rows(change), (low,))
    reached = inner(left_over, precondition(left_over))
    steep = jnp.max(jnp.max(system[4], axis=0, keepdims=True), axis=1, keepdims=True)
    rounds = jnp.where(reached[0, 0] <= bound, 0, 1)
    rounds = jnp.where(steep[0, 0] > STEEP, ROUNDS, rounds)

    def correction(r, z, size, goal):
        def step(state):
            count, _, x, r, p, size = state
            image = apply(p, (high, low))
            energy = inner(p, image)
            length = jnp.where(energy > 0.0, size / energy, 0.0)
            x = x + length * p
            r = r - length * image
            z = precondition(r)
            fresh = inner(r, z)
            p = z + jnp.where(size > 0.0, fresh / size, 0.0) * p
            return (count + 1, jnp.where(fresh[0, 0] > goal, 1, 0), x, r, p, fresh)

        def unfinished(state):
            return jnp.logical_and(state[0] < MOST_STEPS, state[1] > 0)

        return lax.while_loop(unfinished, step, (0, 1, zero, r, z, size))[2]

    def refine(state):
        count, solved = state
        r = residual(solved)
        z = precondition(r)
        size = inner(r, z)
        goal = jnp.minimum(size[0, 0] * (REDUCTION * REDUCTION), bound)
        trial = solved + correction(r, z, size, goal)
        r = residual(trial)
        solved = jnp.where(inner(r, precondition(r)) < size, trial, solved)
        return (count - 1, solved)

    solved = jnp.where(reached < size, x + change, jnp.where(size >= 0.0, x, zero))
    solved = lax.while_loop(lambda state: state[0] > 0, refine, (rounds, solved))[1]
    out_ref[...] = jnp.sum(jnp.where(index == epoch_here, solved, 0.0), axis=0, keepdims=True)


VMEM = pl.BlockSpec(memory_space=pltpu.VMEM)
HBM = pl.BlockSpec(memory_space=pltpu.HBM)
MIB = 2**20


def call(kernel, shape, specs, scratch, vmem, *operands):
    return pl.pallas_call(
        kernel,
        out_shape=pltpu.VMEM(shape, jnp.float32),
        in_specs=specs,
        out_specs=VMEM,
        scratch_shapes=scratch,
        compiler_params=pltpu.CompilerParams(vmem_limit_bytes=vmem * MIB),
    )(*operands)


def solve(mine, other, spread, prior, epochs, width):
    halves = [pltpu.VMEM((epochs * width, width), jnp.bfloat16)] * 2
    tables = [
        pltpu.VMEM((epochs, epochs, width), jnp.float32),
        pltpu.VMEM((5, epochs, width), jnp.float32),
    ]
    high, low, response, system = pl.pallas_call(
        prepare_kernel,
        out_shape=halves + tables,
        in_specs=[VMEM] * 3,
        out_specs=[VMEM] * 4,
        compiler_params=pltpu.CompilerParams(vmem_limit_bytes=8 * MIB),
        cost_estimate=pl.CostEstimate(flops=2**24, bytes_accessed=2**22, transcendentals=0),
    )(mine, spread, prior)
    return pl.pallas_call(
        solve_kernel,
        out_shape=[jax.ShapeDtypeStruct((1, width), jnp.float32)] + halves,
        in_specs=[VMEM] * 6,
        out_specs=[VMEM] * 3,
        input_output_aliases={2: 1, 3: 2},
        compiler_params=pltpu.CompilerParams(vmem_limit_bytes=8 * MIB),
    )(mine, other, high, low, response, system)[0]


def exchange(x, axis, groups=None):
    return lax.all_to_all(
        x, axis, split_axis=0, concat_axis=0, tiled=True, axis_index_groups=groups
    )


def shards(
    ray_basis, delays, ray_station, ray_count, station_var, decay_factor, mode_variance, prior_mean
):
    rays, width = ray_basis.shape[1:]
    stations = station_var.shape[0]
    epochs = lax.axis_size("tm")
    parts = lax.axis_size("sta")
    chips = parts // 2
    scratch = [
        pltpu.SMEM((1, 1), jnp.int32),
        pltpu.SMEM((stations,), jnp.float32),
        pltpu.VMEM((rays, width), jnp.bfloat16),
        pltpu.VMEM((1, rays), jnp.bfloat16),
        pltpu.VMEM((1, rays), jnp.int32),
        pltpu.VMEM((1, width), jnp.float32),
        pltpu.VMEM((rays, width), jnp.bfloat16),
        pltpu.SemaphoreType.DMA((5 + PIECES,)),
    ]
    share = call(
        ray_kernel,
        (parts * SLAB, 1, HALF),
        [HBM] * 6,
        scratch,
        60,
        ray_count,
        station_var,
        ray_basis,
        delays,
        ray_station,
        decay_factor,
    )
    summed = call(
        sum_kernel, (epochs * SLAB, 1, HALF), [VMEM], [], 4, exchange(share, "sta")
    )
    ours = call(
        copy_kernel, (chips, epochs * SLAB, HALF), [VMEM], [], 4, exchange(summed, "tm")
    )
    same_core = [[2 * j + c for j in range(chips)] for c in range(2)]
    ours = ours.reshape(chips * epochs * SLAB, HALF)
    mine = exchange(ours, "sta", same_core).reshape(chips, epochs * SLAB, HALF)
    other = lax.ppermute(mine, "sta", [(i, i + 1 - 2 * (i % 2)) for i in range(parts)])
    return solve(mine, other, mode_variance[None], prior_mean[None], epochs, width)


def solution(mesh):
    placed = (
        P("tm", "sta", None),
        P("tm", "sta"),
        P("tm", "sta"),
        P("tm", "sta"),
        P("sta"),
        P("tm", None),
        P(),
        P(),
    )
    return jax.shard_map(
        shards, mesh=mesh, in_specs=placed, out_specs=P("tm", None), check_vma=False
    )
```

```python
import jax
import jax.numpy as jnp
from jax import lax
from jax.experimental import pallas as pl
from jax.experimental.pallas import tpu as pltpu
from jax.sharding import PartitionSpec as P

HALF = 128
TILE = 8
SLAB = TILE + 1
EXTRAS = 6
TOLERANCE = 2e-5
COARSE = 5e-2
SHORT_STEPS = 24
STEEP = 16.0
ROUNDS = 3
REDUCTION = 1e-4
PIECES = 4
MOST_STEPS = 1000


def ray_kernel(
    count_hbm,
    var_hbm,
    basis_hbm,
    delay_hbm,
    station_hbm,
    decay_hbm,
    out_ref,
    count_ref,
    var_ref,
    basis_ref,
    delay_ref,
    station_ref,
    decay_ref,
    weighted,
    arrived,
):
    rays = basis_ref.shape[0]
    stations = var_ref.shape[0]
    small = [
        pltpu.make_async_copy(source, target, arrived.at[k])
        for k, (source, target) in enumerate(
            (
                (station_hbm, station_ref),
                (var_hbm, var_ref),
                (count_hbm, count_ref),
                (delay_hbm, delay_ref),
                (decay_hbm, decay_ref),
            )
        )
    ]
    large = [
        pltpu.make_async_copy(
            basis_hbm.at[0, pl.ds(k * rays // PIECES, rays // PIECES)],
            basis_ref.at[pl.ds(k * rays // PIECES, rays // PIECES)],
            arrived.at[len(small) + k],
        )
        for k in range(PIECES)
    ]
    for copy in small + large:
        copy.start()
    shard = lax.axis_index("sta")
    for copy in small:
        copy.wait()
    local = station_ref[...] - shard * stations
    variance = jnp.ones(local.shape, jnp.float32)
    for k in range(stations):
        variance = jnp.where(local == k, var_ref[k], variance)
    slot = lax.broadcasted_iota(jnp.int32, local.shape, 1)
    weight = jnp.where(slot < count_ref[0, 0], 1.0 / variance, 0.0)
    for start in range(0, rays, HALF):
        if start % (rays // PIECES) == 0:
            large[start * PIECES // rays].wait()
        rows = slice(start, start + HALF)
        column = jnp.broadcast_to(weight[:, rows], (HALF, HALF)).T
        for lane in (0, HALF):
            lanes = slice(lane, lane + HALF)
            block = basis_ref[rows, lanes].astype(jnp.float32)
            weighted[rows, lanes] = (block * column).astype(jnp.bfloat16)
    scaled = weighted[...]
    information = lax.dot_general(
        scaled, basis_ref[...], (((0,), (0,)), ((), ())), preferred_element_type=jnp.float32
    )
    drive = jnp.dot(delay_ref[...], scaled, preferred_element_type=jnp.float32)
    first = information[:HALF, :HALF]
    second = information[HALF:, HALF:]
    row = lax.broadcasted_iota(jnp.int32, (HALF, HALF), 0)
    col = lax.broadcasted_iota(jnp.int32, (HALF, HALF), 1)
    diagonals = [
        jnp.sum(jnp.where(row == col, block, 0.0), axis=0, keepdims=True) for block in (first, second)
    ]
    triangles = jnp.where(col >= row, first, second)
    corner = information[:HALF, HALF:]
    own = jnp.where(shard == 0, decay_ref[...], 0.0)
    extras = [drive[:, :HALF], drive[:, HALF:], *diagonals, own[:, :HALF], own[:, HALF:]]
    blank = jnp.zeros((1, HALF), jnp.float32)
    chips = HALF // TILE
    for j in range(chips):
        for c, block in ((0, triangles), (1, corner)):
            base = (2 * j + c) * SLAB
            out_ref[base : base + TILE, 0, :] = block[j * TILE : j * TILE + TILE, :]
            out_ref[base + TILE, :, :] = blank
    for k, extra in enumerate(extras):
        j = lax.rem(lax.axis_index("tm") + k, chips)
        for c in range(2):
            out_ref[(2 * j + c) * SLAB + TILE, :, :] = extra


def sum_kernel(parts_ref, out_ref):
    total = parts_ref[0:TILE, 0, :]
    extra = parts_ref[TILE, :, :]
    for k in range(1, parts_ref.shape[0] // SLAB):
        base = k * SLAB
        total = total + parts_ref[base : base + TILE, 0, :]
        extra = extra + parts_ref[base + TILE, :, :]
    for k in range(out_ref.shape[0] // SLAB):
        base = k * SLAB
        out_ref[base : base + TILE, 0, :] = total
        out_ref[base + TILE, :, :] = extra


def copy_kernel(rows_ref, out_ref):
    chips = out_ref.shape[0]
    epochs = rows_ref.shape[0] // SLAB
    here = lax.axis_index("sta") // 2
    tiles = [rows_ref[k * SLAB : k * SLAB + TILE, 0, :] for k in range(epochs)]
    rows = [
        rows_ref[lax.rem(here - k + epochs, epochs) * SLAB + TILE, :, :] for k in range(EXTRAS)
    ]
    rows.append(jnp.zeros((TILE - EXTRAS, HALF), jnp.float32))
    tiles.append(jnp.concatenate(rows, axis=0))
    for j in range(chips):
        for k, tile in enumerate(tiles):
            out_ref[j, k * TILE : k * TILE + TILE, :] = tile


def whole(slabs_ref, e):
    place = pl.multiple_of(e * TILE, TILE)
    chips = slabs_ref.shape[0]
    return jnp.concatenate([slabs_ref[j, pl.ds(place, TILE), :] for j in range(chips)], axis=0)


def diagonal_blocks(triangles):
    row = lax.broadcasted_iota(jnp.int32, (HALF, HALF), 0)
    col = lax.broadcasted_iota(jnp.int32, (HALF, HALF), 1)
    turned = triangles.T
    return (
        jnp.where(row == col, 0.0, jnp.where(col > row, triangles, turned)),
        jnp.where(row == col, 0.0, jnp.where(col < row, triangles, turned)),
    )


def unpack(slabs_ref, triangles, high, low, epochs, width):
    def one(e, carry):
        block = whole(slabs_ref, e)
        pair = diagonal_blocks(block) if triangles else (block, block.T)
        for r in range(2):
            rows = pl.ds(pl.multiple_of(e * width + r * HALF, HALF), HALF)
            lane = (r if triangles else 1 - r) * HALF
            upper = pair[r].astype(jnp.bfloat16)
            high[rows, lane : lane + HALF] = upper
            low[rows, lane : lane + HALF] = (pair[r] - upper.astype(jnp.float32)).astype(jnp.bfloat16)
        return carry

    lax.fori_loop(0, epochs, one, 0, unroll=16)


def prepare_kernel(mine_ref, spread_ref, prior_ref, high, low, response, system):
    epochs, _, width = response.shape
    core = lax.rem(lax.axis_index("sta"), 2)
    pl.when(core == 0)(lambda: unpack(mine_ref, True, high, low, epochs, width))
    pl.when(core == 1)(lambda: unpack(mine_ref, False, high, low, epochs, width))

    def extra_half(k):
        row = epochs * TILE + k
        chips = mine_ref.shape[0]
        return jnp.concatenate(
            [mine_ref[(e + k) % chips, row : row + 1, :] for e in range(epochs)], axis=0
        )

    def extra(k):
        return jnp.concatenate([extra_half(k), extra_half(k + 1)], axis=1)

    drive, diagonal, decay = extra(0), extra(2), extra(4)
    inverse_noise = 1.0 / ((1.0 - decay * decay) * spread_ref[...])
    index = lax.broadcasted_iota(jnp.int32, (epochs, width), 0)
    pull = decay * inverse_noise
    link_back = jnp.where(index == 0, 0.0, pull)
    link = jnp.where(index == epochs - 1, 0.0, pltpu.roll(pull, epochs - 1, 0))
    carried = jnp.where(index == epochs - 1, 0.0, pltpu.roll(decay * pull, epochs - 1, 0))
    middle = inverse_noise + carried + diagonal
    right = drive + jnp.where(index == 0, pull * prior_ref[...], 0.0)
    system[0] = middle
    system[1] = link
    system[2] = link_back
    system[3] = right
    system[4] = diagonal * spread_ref[...]

    at = lambda x, e: x[e : e + 1, :]
    ahead = [at(middle, 0)]
    up = []
    for e in range(epochs - 1):
        up.append(at(link, e) / ahead[e])
        ahead.append(at(middle, e + 1) - at(link, e) * up[e])
    behind = at(middle, epochs - 1)
    down = [None] * epochs
    centre = [None] * epochs
    centre[epochs - 1] = 1.0 / ahead[epochs - 1]
    for e in reversed(range(epochs - 1)):
        down[e] = at(link, e) / behind
        reduced = at(link, e) * down[e]
        behind = at(middle, e) - reduced
        centre[e] = 1.0 / (ahead[e] - reduced)
    below = jnp.zeros((epochs, width), jnp.float32)
    for e in range(epochs):
        if e:
            below = below * down[e - 1]
        below = jnp.where(index == e, centre[e], below)
        response[e] = below
    above = jnp.where(index == epochs - 1, centre[epochs - 1], 0.0)
    for e in reversed(range(epochs - 1)):
        above = above * up[e]
        response[e] = response[e] + above
        above = jnp.where(index == e, centre[e], above)


def solve_kernel(mine_ref, other_ref, high_in, low_in, response, system, out_ref, high, low):
    epochs, _, width = response.shape
    core = lax.rem(lax.axis_index("sta"), 2)
    epoch_here = lax.axis_index("tm")
    pl.when(core == 0)(lambda: unpack(other_ref, False, high, low, epochs, width))
    pl.when(core == 1)(lambda: unpack(other_ref, True, high, low, epochs, width))
    middle, link, link_back, right = (system[k] for k in range(4))
    index = lax.broadcasted_iota(jnp.int32, (epochs, width), 0)
    at = lambda x, e: x[e : e + 1, :]

    def precondition(r):
        total = at(r, 0) * response[0]
        for e in range(1, epochs):
            total = total + at(r, e) * response[e]
        return total

    def spread_rows(p):
        upper = p.astype(jnp.bfloat16).astype(jnp.float32)
        rest = p - upper
        which = lax.rem(lax.broadcasted_iota(jnp.int32, (2 * TILE, width), 0), TILE)
        lefts = []
        for g in range(0, epochs, TILE):
            both = jnp.concatenate([upper[g : g + TILE], rest[g : g + TILE]], axis=0)
            pieces = [jnp.where(which == e, both, 0.0).astype(jnp.bfloat16) for e in range(TILE)]
            lefts.append(jnp.concatenate(pieces, axis=1))
        return lefts

    def products(lefts, halves):
        groups = []
        for k, left in enumerate(lefts):
            rows = slice(k * TILE * width, (k + 1) * TILE * width)
            by = sum(jnp.dot(left, h[rows], preferred_element_type=jnp.float32) for h in halves)
            groups.append(by[:TILE] + by[TILE:])
        return jnp.concatenate(groups, axis=0)

    def near(p):
        return (
            middle * p
            - link * pltpu.roll(p, epochs - 1, 0)
            - link_back * pltpu.roll(p, 1, 0)
        )

    def apply(p, halves):
        return near(p) + products(spread_rows(p), halves)

    def residual(x):
        def one(e, total):
            mine = whole(mine_ref, e)
            other = whole(other_ref, e)
            corner = jnp.where(core == 0, other, mine)
            first, second = diagonal_blocks(jnp.where(core == 0, mine, other))
            kept = jnp.where(index == e, x, 0.0)
            left, right_half = kept[:, :HALF], kept[:, HALF:]
            dot = lambda u, m: jnp.dot(
                u, m, precision=lax.Precision.HIGHEST, preferred_element_type=jnp.float32
            )
            lower = dot(left, first) + dot(right_half, corner.T)
            upper = dot(left, corner) + dot(right_half, second)
            return total + jnp.concatenate([lower, upper], axis=1)

        return right - near(x) - lax.fori_loop(0, epochs, one, zero)

    def inner(a, b):
        return jnp.sum(jnp.sum(a * b, axis=0, keepdims=True), axis=1, keepdims=True)

    zero = jnp.zeros((epochs, width), jnp.float32)
    none = jnp.zeros((1, 1), jnp.float32)

    def iterate(halves, most, bound, x, r, z, p, path, before, length):
        def unfinished(state):
            return jnp.logical_and(state[0] < most, state[1] > 0)

        def step(state):
            count, _, x, r, z, p, path, before, length = state
            size = inner(r, z)
            again = jnp.where(size[0, 0] > bound, 1, 0)
            image = apply(z, halves)
            ratio = jnp.where(before > 0.0, size / before, 0.0)
            past = jnp.where(length > 0.0, ratio * size / length, 0.0)
            energy = inner(z, image) - past
            length = jnp.where(energy > 0.0, size / energy, 0.0)
            p = z + ratio * p
            path = image + ratio * path
            x = x + length * p
            r = r - length * path
            z = precondition(r)
            return (count + 1, again, x, r, z, p, path, size, length)

        return lax.while_loop(unfinished, step, (0, 1, x, r, z, p, path, before, length))[2:]

    start = precondition(right)
    size = inner(right, start)[0, 0]
    bound = size * (TOLERANCE * TOLERANCE)
    coarse = size * (COARSE * COARSE)
    x, r, z, *rest = iterate(
        (high, low), MOST_STEPS, coarse, zero, right, start, zero, zero, none, none
    )
    size = inner(r, z)
    change, left_over, *_ = iterate((high,), SHORT_STEPS, bound, zero, r, z, *rest)
    left_over = left_over - products(spread_rows(change), (low,))
    reached = inner(left_over, precondition(left_over))
    steep = jnp.max(jnp.max(system[4], axis=0, keepdims=True), axis=1, keepdims=True)
    rounds = jnp.where(reached[0, 0] <= bound, 0, 1)
    rounds = jnp.where(steep[0, 0] > STEEP, ROUNDS, rounds)

    def correction(r, z, size, goal):
        def step(state):
            count, _, x, r, p, size = state
            image = apply(p, (high, low))
            energy = inner(p, image)
            length = jnp.where(energy > 0.0, size / energy, 0.0)
            x = x + length * p
            r = r - length * image
            z = precondition(r)
            fresh = inner(r, z)
            p = z + jnp.where(size > 0.0, fresh / size, 0.0) * p
            return (count + 1, jnp.where(fresh[0, 0] > goal, 1, 0), x, r, p, fresh)

        def unfinished(state):
            return jnp.logical_and(state[0] < MOST_STEPS, state[1] > 0)

        return lax.while_loop(unfinished, step, (0, 1, zero, r, z, size))[2]

    def refine(state):
        count, solved = state
        r = residual(solved)
        z = precondition(r)
        size = inner(r, z)
        goal = jnp.minimum(size[0, 0] * (REDUCTION * REDUCTION), bound)
        trial = solved + correction(r, z, size, goal)
        r = residual(trial)
        solved = jnp.where(inner(r, precondition(r)) < size, trial, solved)
        return (count - 1, solved)

    solved = jnp.where(reached < size, x + change, jnp.where(size >= 0.0, x, zero))
    solved = lax.while_loop(lambda state: state[0] > 0, refine, (rounds, solved))[1]
    out_ref[...] = jnp.sum(jnp.where(index == epoch_here, solved, 0.0), axis=0, keepdims=True)


VMEM = pl.BlockSpec(memory_space=pltpu.VMEM)
HBM = pl.BlockSpec(memory_space=pltpu.HBM)
MIB = 2**20


def call(kernel, shape, specs, scratch, vmem, *operands):
    return pl.pallas_call(
        kernel,
        out_shape=pltpu.VMEM(shape, jnp.float32),
        in_specs=specs,
        out_specs=VMEM,
        scratch_shapes=scratch,
        compiler_params=pltpu.CompilerParams(vmem_limit_bytes=vmem * MIB),
    )(*operands)


def solve(mine, other, spread, prior, epochs, width):
    halves = [pltpu.VMEM((epochs * width, width), jnp.bfloat16)] * 2
    tables = [
        pltpu.VMEM((epochs, epochs, width), jnp.float32),
        pltpu.VMEM((5, epochs, width), jnp.float32),
    ]
    high, low, response, system = pl.pallas_call(
        prepare_kernel,
        out_shape=halves + tables,
        in_specs=[VMEM] * 3,
        out_specs=[VMEM] * 4,
        compiler_params=pltpu.CompilerParams(vmem_limit_bytes=8 * MIB),
        cost_estimate=pl.CostEstimate(flops=2**24, bytes_accessed=2**22, transcendentals=0),
    )(mine, spread, prior)
    return pl.pallas_call(
        solve_kernel,
        out_shape=[jax.ShapeDtypeStruct((1, width), jnp.float32)] + halves,
        in_specs=[VMEM] * 6,
        out_specs=[VMEM] * 3,
        input_output_aliases={2: 1, 3: 2},
        compiler_params=pltpu.CompilerParams(vmem_limit_bytes=8 * MIB),
    )(mine, other, high, low, response, system)[0]


def exchange(x, axis, groups=None):
    return lax.all_to_all(
        x, axis, split_axis=0, concat_axis=0, tiled=True, axis_index_groups=groups
    )


def shards(
    ray_basis, delays, ray_station, ray_count, station_var, decay_factor, mode_variance, prior_mean
):
    rays, width = ray_basis.shape[1:]
    stations = station_var.shape[0]
    epochs = lax.axis_size("tm")
    parts = lax.axis_size("sta")
    chips = parts // 2
    tall = (epochs + 1) * TILE
    scratch = [
        pltpu.SMEM((1, 1), jnp.int32),
        pltpu.SMEM((stations,), jnp.float32),
        pltpu.VMEM((rays, width), jnp.bfloat16),
        pltpu.VMEM((1, rays), jnp.bfloat16),
        pltpu.VMEM((1, rays), jnp.int32),
        pltpu.VMEM((1, width), jnp.float32),
        pltpu.VMEM((rays, width), jnp.bfloat16),
        pltpu.SemaphoreType.DMA((5 + PIECES,)),
    ]
    share = call(
        ray_kernel,
        (parts * SLAB, 1, HALF),
        [HBM] * 6,
        scratch,
        60,
        ray_count,
        station_var,
        ray_basis,
        delays,
        ray_station,
        decay_factor,
    )
    summed = call(
        sum_kernel, (epochs * SLAB, 1, HALF), [VMEM], [], 4, exchange(share, "sta")
    )
    ours = call(
        copy_kernel, (chips, tall, HALF), [VMEM], [], 4, exchange(summed, "tm")
    )
    same_core = [[2 * j + c for j in range(chips)] for c in range(2)]
    ours = ours.reshape(chips * tall, HALF)
    mine = exchange(ours, "sta", same_core).reshape(chips, tall, HALF)
    other = lax.ppermute(mine, "sta", [(i, i + 1 - 2 * (i % 2)) for i in range(parts)])
    return solve(mine, other, mode_variance[None], prior_mean[None], epochs, width)


def solution(mesh):
    placed = (
        P("tm", "sta", None),
        P("tm", "sta"),
        P("tm", "sta"),
        P("tm", "sta"),
        P("sta"),
        P("tm", None),
        P(),
        P(),
    )
    return jax.shard_map(
        shards, mesh=mesh, in_specs=placed, out_specs=P("tm", None), check_vma=False
    )
```

```python
import jax
import jax.numpy as jnp
from jax import lax
from jax.experimental import pallas as pl
from jax.experimental.pallas import tpu as pltpu
from jax.sharding import PartitionSpec as P

HALF = 128
TILE = 8
SLAB = TILE + 1
EXTRAS = 6
TOLERANCE = 2e-5
COARSE = 5e-2
SHORT_STEPS = 24
STEEP = 16.0
ROUNDS = 3
REDUCTION = 1e-4
PIECES = 4
MOST_STEPS = 1000


def ray_kernel(
    count_hbm,
    var_hbm,
    basis_hbm,
    delay_hbm,
    station_hbm,
    decay_hbm,
    out_ref,
    count_ref,
    var_ref,
    basis_ref,
    delay_ref,
    station_ref,
    decay_ref,
    weighted,
    arrived,
):
    rays = basis_ref.shape[0]
    stations = var_ref.shape[0]
    small = [
        pltpu.make_async_copy(source, target, arrived.at[k])
        for k, (source, target) in enumerate(
            (
                (station_hbm, station_ref),
                (var_hbm, var_ref),
                (count_hbm, count_ref),
                (delay_hbm, delay_ref),
                (decay_hbm, decay_ref),
            )
        )
    ]
    large = [
        pltpu.make_async_copy(
            basis_hbm.at[0, pl.ds(k * rays // PIECES, rays // PIECES)],
            basis_ref.at[pl.ds(k * rays // PIECES, rays // PIECES)],
            arrived.at[len(small) + k],
        )
        for k in range(PIECES)
    ]
    for copy in small + large:
        copy.start()
    shard = lax.axis_index("sta")
    for copy in small:
        copy.wait()
    local = station_ref[...] - shard * stations
    variance = jnp.ones(local.shape, jnp.float32)
    for k in range(stations):
        variance = jnp.where(local == k, var_ref[k], variance)
    slot = lax.broadcasted_iota(jnp.int32, local.shape, 1)
    weight = jnp.where(slot < count_ref[0, 0], 1.0 / variance, 0.0)
    for start in range(0, rays, HALF):
        if start % (rays // PIECES) == 0:
            large[start * PIECES // rays].wait()
        rows = slice(start, start + HALF)
        column = jnp.broadcast_to(weight[:, rows], (HALF, HALF)).T
        for lane in (0, HALF):
            lanes = slice(lane, lane + HALF)
            block = basis_ref[rows, lanes].astype(jnp.float32)
            weighted[rows, lanes] = (block * column).astype(jnp.bfloat16)
    scaled = weighted[...]
    information = lax.dot_general(
        scaled, basis_ref[...], (((0,), (0,)), ((), ())), preferred_element_type=jnp.float32
    )
    drive = jnp.dot(delay_ref[...], scaled, preferred_element_type=jnp.float32)
    first = information[:HALF, :HALF]
    second = information[HALF:, HALF:]
    row = lax.broadcasted_iota(jnp.int32, (HALF, HALF), 0)
    col = lax.broadcasted_iota(jnp.int32, (HALF, HALF), 1)
    diagonals = [
        jnp.sum(jnp.where(row == col, block, 0.0), axis=0, keepdims=True) for block in (first, second)
    ]
    triangles = jnp.where(col >= row, first, second)
    corner = information[:HALF, HALF:]
    own = jnp.where(shard == 0, decay_ref[...], 0.0)
    extras = [drive[:, :HALF], drive[:, HALF:], *diagonals, own[:, :HALF], own[:, HALF:]]
    blank = jnp.zeros((1, HALF), jnp.float32)
    chips = HALF // TILE
    for j in range(chips):
        for c, block in ((0, triangles), (1, corner)):
            base = (2 * j + c) * SLAB
            out_ref[base : base + TILE, 0, :] = block[j * TILE : j * TILE + TILE, :]
            out_ref[base + TILE, :, :] = blank
    for k, extra in enumerate(extras):
        j = lax.rem(lax.axis_index("tm") + k, chips)
        for c in range(2):
            out_ref[(2 * j + c) * SLAB + TILE, :, :] = extra


def sum_kernel(parts_ref, out_ref):
    total = parts_ref[0:TILE, 0, :]
    extra = parts_ref[TILE, :, :]
    for k in range(1, parts_ref.shape[0] // SLAB):
        base = k * SLAB
        total = total + parts_ref[base : base + TILE, 0, :]
        extra = extra + parts_ref[base + TILE, :, :]
    for k in range(out_ref.shape[0] // SLAB):
        base = k * SLAB
        out_ref[base : base + TILE, 0, :] = total
        out_ref[base + TILE, :, :] = extra


def copy_kernel(rows_ref, out_ref):
    chips = out_ref.shape[0]
    epochs = rows_ref.shape[0] // SLAB
    here = lax.axis_index("sta") // 2
    tiles = [rows_ref[k * SLAB : k * SLAB + TILE, 0, :] for k in range(epochs)]
    rows = [
        rows_ref[lax.rem(here - k + epochs, epochs) * SLAB + TILE, :, :] for k in range(EXTRAS)
    ]
    rows.append(jnp.zeros((TILE - EXTRAS, HALF), jnp.float32))
    tiles.append(jnp.concatenate(rows, axis=0))
    for j in range(chips):
        for k, tile in enumerate(tiles):
            out_ref[j, k * TILE : k * TILE + TILE, :] = tile


def whole(slabs_ref, e):
    place = pl.multiple_of(e * TILE, TILE)
    chips = slabs_ref.shape[0]
    return jnp.concatenate([slabs_ref[j, pl.ds(place, TILE), :] for j in range(chips)], axis=0)


def diagonal_blocks(triangles):
    row = lax.broadcasted_iota(jnp.int32, (HALF, HALF), 0)
    col = lax.broadcasted_iota(jnp.int32, (HALF, HALF), 1)
    turned = triangles.T
    return (
        jnp.where(row == col, 0.0, jnp.where(col > row, triangles, turned)),
        jnp.where(row == col, 0.0, jnp.where(col < row, triangles, turned)),
    )


def unpack(slabs_ref, triangles, high, low, epochs, width):
    def one(e, carry):
        block = whole(slabs_ref, e)
        pair = diagonal_blocks(block) if triangles else (block, block.T)
        for r in range(2):
            rows = pl.ds(pl.multiple_of(e * width + r * HALF, HALF), HALF)
            lane = (r if triangles else 1 - r) * HALF
            upper = pair[r].astype(jnp.bfloat16)
            high[rows, lane : lane + HALF] = upper
            low[rows, lane : lane + HALF] = (pair[r] - upper.astype(jnp.float32)).astype(jnp.bfloat16)
        return carry

    lax.fori_loop(0, epochs, one, 0, unroll=16)


def prepare_kernel(mine_ref, spread_ref, prior_ref, high, low, response, system):
    epochs, _, width = response.shape
    core = lax.rem(lax.axis_index("sta"), 2)
    pl.when(core == 0)(lambda: unpack(mine_ref, True, high, low, epochs, width))
    pl.when(core == 1)(lambda: unpack(mine_ref, False, high, low, epochs, width))

    def extra_half(k):
        row = epochs * TILE + k
        chips = mine_ref.shape[0]
        return jnp.concatenate(
            [mine_ref[(e + k) % chips, row : row + 1, :] for e in range(epochs)], axis=0
        )

    def extra(k):
        return jnp.concatenate([extra_half(k), extra_half(k + 1)], axis=1)

    drive, diagonal, decay = extra(0), extra(2), extra(4)
    inverse_noise = 1.0 / ((1.0 - decay * decay) * spread_ref[...])
    index = lax.broadcasted_iota(jnp.int32, (epochs, width), 0)
    pull = decay * inverse_noise
    link_back = jnp.where(index == 0, 0.0, pull)
    link = jnp.where(index == epochs - 1, 0.0, pltpu.roll(pull, epochs - 1, 0))
    carried = jnp.where(index == epochs - 1, 0.0, pltpu.roll(decay * pull, epochs - 1, 0))
    middle = inverse_noise + carried + diagonal
    right = drive + jnp.where(index == 0, pull * prior_ref[...], 0.0)
    system[0] = middle
    system[1] = link
    system[2] = link_back
    system[3] = right

    at = lambda x, e: x[e : e + 1, :]
    ahead = [at(middle, 0)]
    up = []
    for e in range(epochs - 1):
        up.append(at(link, e) / ahead[e])
        ahead.append(at(middle, e + 1) - at(link, e) * up[e])
    behind = at(middle, epochs - 1)
    down = [None] * epochs
    centre = [None] * epochs
    centre[epochs - 1] = 1.0 / ahead[epochs - 1]
    for e in reversed(range(epochs - 1)):
        down[e] = at(link, e) / behind
        reduced = at(link, e) * down[e]
        behind = at(middle, e) - reduced
        centre[e] = 1.0 / (ahead[e] - reduced)
    below = jnp.zeros((epochs, width), jnp.float32)
    for e in range(epochs):
        if e:
            below = below * down[e - 1]
        below = jnp.where(index == e, centre[e], below)
        response[e] = below
    above = jnp.where(index == epochs - 1, centre[epochs - 1], 0.0)
    for e in reversed(range(epochs - 1)):
        above = above * up[e]
        response[e] = response[e] + above
        above = jnp.where(index == e, centre[e], above)
    start = at(right, 0) * response[0]
    for e in range(1, epochs):
        start = start + at(right, e) * response[e]
    total = jnp.sum(jnp.sum(right * start, axis=0, keepdims=True), axis=1, keepdims=True)
    peak = jnp.max(
        jnp.max(diagonal * spread_ref[...], axis=0, keepdims=True), axis=1, keepdims=True
    )
    system[4] = start
    system[5] = jnp.where(index == 0, total, peak)


def solve_kernel(mine_ref, other_ref, high_in, low_in, response, system, out_ref, high, low):
    epochs, _, width = response.shape
    core = lax.rem(lax.axis_index("sta"), 2)
    epoch_here = lax.axis_index("tm")
    pl.when(core == 0)(lambda: unpack(other_ref, False, high, low, epochs, width))
    pl.when(core == 1)(lambda: unpack(other_ref, True, high, low, epochs, width))
    middle, link, link_back, right = (system[k] for k in range(4))
    index = lax.broadcasted_iota(jnp.int32, (epochs, width), 0)
    at = lambda x, e: x[e : e + 1, :]

    def precondition(r):
        total = at(r, 0) * response[0]
        for e in range(1, epochs):
            total = total + at(r, e) * response[e]
        return total

    def spread_rows(p):
        upper = p.astype(jnp.bfloat16).astype(jnp.float32)
        rest = p - upper
        which = lax.rem(lax.broadcasted_iota(jnp.int32, (2 * TILE, width), 0), TILE)
        lefts = []
        for g in range(0, epochs, TILE):
            both = jnp.concatenate([upper[g : g + TILE], rest[g : g + TILE]], axis=0)
            pieces = [jnp.where(which == e, both, 0.0).astype(jnp.bfloat16) for e in range(TILE)]
            lefts.append(jnp.concatenate(pieces, axis=1))
        return lefts

    def products(lefts, halves):
        groups = []
        for k, left in enumerate(lefts):
            rows = slice(k * TILE * width, (k + 1) * TILE * width)
            by = sum(jnp.dot(left, h[rows], preferred_element_type=jnp.float32) for h in halves)
            groups.append(by[:TILE] + by[TILE:])
        return jnp.concatenate(groups, axis=0)

    def near(p):
        return (
            middle * p
            - link * pltpu.roll(p, epochs - 1, 0)
            - link_back * pltpu.roll(p, 1, 0)
        )

    def apply(p, halves):
        return near(p) + products(spread_rows(p), halves)

    def residual(x):
        def one(e, total):
            mine = whole(mine_ref, e)
            other = whole(other_ref, e)
            corner = jnp.where(core == 0, other, mine)
            first, second = diagonal_blocks(jnp.where(core == 0, mine, other))
            kept = jnp.where(index == e, x, 0.0)
            left, right_half = kept[:, :HALF], kept[:, HALF:]
            dot = lambda u, m: jnp.dot(
                u, m, precision=lax.Precision.HIGHEST, preferred_element_type=jnp.float32
            )
            lower = dot(left, first) + dot(right_half, corner.T)
            upper = dot(left, corner) + dot(right_half, second)
            return total + jnp.concatenate([lower, upper], axis=1)

        return right - near(x) - lax.fori_loop(0, epochs, one, zero)

    def inner(a, b):
        return jnp.sum(jnp.sum(a * b, axis=0, keepdims=True), axis=1, keepdims=True)

    zero = jnp.zeros((epochs, width), jnp.float32)
    none = jnp.zeros((1, 1), jnp.float32)

    def iterate(halves, most, bound, x, r, z, p, path, before, length):
        def unfinished(state):
            return jnp.logical_and(state[0] < most, state[1] > 0)

        def step(state):
            count, _, x, r, z, p, path, before, length = state
            size = inner(r, z)
            again = jnp.where(size[0, 0] > bound, 1, 0)
            image = apply(z, halves)
            ratio = jnp.where(before > 0.0, size / before, 0.0)
            past = jnp.where(length > 0.0, ratio * size / length, 0.0)
            energy = inner(z, image) - past
            length = jnp.where(energy > 0.0, size / energy, 0.0)
            p = z + ratio * p
            path = image + ratio * path
            x = x + length * p
            r = r - length * path
            z = precondition(r)
            return (count + 1, again, x, r, z, p, path, size, length)

        return lax.while_loop(unfinished, step, (0, 1, x, r, z, p, path, before, length))[2:]

    start = system[4]
    size = system[5, 0:1, 0:1][0, 0]
    bound = size * (TOLERANCE * TOLERANCE)
    coarse = size * (COARSE * COARSE)
    x, r, z, *rest = iterate(
        (high, low), MOST_STEPS, coarse, zero, right, start, zero, zero, none, none
    )
    size = inner(r, z)
    change, left_over, *_ = iterate((high,), SHORT_STEPS, bound, zero, r, z, *rest)
    left_over = left_over - products(spread_rows(change), (low,))
    reached = inner(left_over, precondition(left_over))
    steep = system[5, 1:2, 0:1]
    rounds = jnp.where(reached[0, 0] <= bound, 0, 1)
    rounds = jnp.where(steep[0, 0] > STEEP, ROUNDS, rounds)

    def correction(r, z, size, goal):
        def step(state):
            count, _, x, r, p, size = state
            image = apply(p, (high, low))
            energy = inner(p, image)
            length = jnp.where(energy > 0.0, size / energy, 0.0)
            x = x + length * p
            r = r - length * image
            z = precondition(r)
            fresh = inner(r, z)
            p = z + jnp.where(size > 0.0, fresh / size, 0.0) * p
            return (count + 1, jnp.where(fresh[0, 0] > goal, 1, 0), x, r, p, fresh)

        def unfinished(state):
            return jnp.logical_and(state[0] < MOST_STEPS, state[1] > 0)

        return lax.while_loop(unfinished, step, (0, 1, zero, r, z, size))[2]

    def refine(state):
        count, solved = state
        r = residual(solved)
        z = precondition(r)
        size = inner(r, z)
        goal = jnp.minimum(size[0, 0] * (REDUCTION * REDUCTION), bound)
        trial = solved + correction(r, z, size, goal)
        r = residual(trial)
        solved = jnp.where(inner(r, precondition(r)) < size, trial, solved)
        return (count - 1, solved)

    solved = jnp.where(reached < size, x + change, jnp.where(size >= 0.0, x, zero))
    solved = lax.while_loop(lambda state: state[0] > 0, refine, (rounds, solved))[1]
    out_ref[...] = jnp.sum(jnp.where(index == epoch_here, solved, 0.0), axis=0, keepdims=True)


VMEM = pl.BlockSpec(memory_space=pltpu.VMEM)
HBM = pl.BlockSpec(memory_space=pltpu.HBM)
MIB = 2**20


def call(kernel, shape, specs, scratch, vmem, *operands):
    return pl.pallas_call(
        kernel,
        out_shape=pltpu.VMEM(shape, jnp.float32),
        in_specs=specs,
        out_specs=VMEM,
        scratch_shapes=scratch,
        compiler_params=pltpu.CompilerParams(vmem_limit_bytes=vmem * MIB),
    )(*operands)


def solve(mine, other, spread, prior, epochs, width):
    halves = [pltpu.VMEM((epochs * width, width), jnp.bfloat16)] * 2
    tables = [
        pltpu.VMEM((epochs, epochs, width), jnp.float32),
        pltpu.VMEM((6, epochs, width), jnp.float32),
    ]
    high, low, response, system = pl.pallas_call(
        prepare_kernel,
        out_shape=halves + tables,
        in_specs=[VMEM] * 3,
        out_specs=[VMEM] * 4,
        compiler_params=pltpu.CompilerParams(vmem_limit_bytes=8 * MIB),
        cost_estimate=pl.CostEstimate(flops=2**24, bytes_accessed=2**22, transcendentals=0),
    )(mine, spread, prior)
    return pl.pallas_call(
        solve_kernel,
        out_shape=[jax.ShapeDtypeStruct((1, width), jnp.float32)] + halves,
        in_specs=[VMEM] * 6,
        out_specs=[VMEM] * 3,
        input_output_aliases={2: 1, 3: 2},
        compiler_params=pltpu.CompilerParams(vmem_limit_bytes=8 * MIB),
    )(mine, other, high, low, response, system)[0]


def exchange(x, axis, groups=None):
    return lax.all_to_all(
        x, axis, split_axis=0, concat_axis=0, tiled=True, axis_index_groups=groups
    )


def shards(
    ray_basis, delays, ray_station, ray_count, station_var, decay_factor, mode_variance, prior_mean
):
    rays, width = ray_basis.shape[1:]
    stations = station_var.shape[0]
    epochs = lax.axis_size("tm")
    parts = lax.axis_size("sta")
    chips = parts // 2
    tall = (epochs + 1) * TILE
    scratch = [
        pltpu.SMEM((1, 1), jnp.int32),
        pltpu.SMEM((stations,), jnp.float32),
        pltpu.VMEM((rays, width), jnp.bfloat16),
        pltpu.VMEM((1, rays), jnp.bfloat16),
        pltpu.VMEM((1, rays), jnp.int32),
        pltpu.VMEM((1, width), jnp.float32),
        pltpu.VMEM((rays, width), jnp.bfloat16),
        pltpu.SemaphoreType.DMA((5 + PIECES,)),
    ]
    share = call(
        ray_kernel,
        (parts * SLAB, 1, HALF),
        [HBM] * 6,
        scratch,
        60,
        ray_count,
        station_var,
        ray_basis,
        delays,
        ray_station,
        decay_factor,
    )
    summed = call(
        sum_kernel, (epochs * SLAB, 1, HALF), [VMEM], [], 4, exchange(share, "sta")
    )
    ours = call(
        copy_kernel, (chips, tall, HALF), [VMEM], [], 4, exchange(summed, "tm")
    )
    same_core = [[2 * j + c for j in range(chips)] for c in range(2)]
    ours = ours.reshape(chips * tall, HALF)
    mine = exchange(ours, "sta", same_core).reshape(chips, tall, HALF)
    other = lax.ppermute(mine, "sta", [(i, i + 1 - 2 * (i % 2)) for i in range(parts)])
    return solve(mine, other, mode_variance[None], prior_mean[None], epochs, width)


def solution(mesh):
    placed = (
        P("tm", "sta", None),
        P("tm", "sta"),
        P("tm", "sta"),
        P("tm", "sta"),
        P("sta"),
        P("tm", None),
        P(),
        P(),
    )
    return jax.shard_map(
        shards, mesh=mesh, in_specs=placed, out_specs=P("tm", None), check_vma=False
    )
```
